768 devices in a mesh: gx: 24 (over y_lo, z), gy: 8 (over y_hi, core), gz: 4 (over x).
Axes of the slice: x: 4, y: 8 (y_hi: 4, y_lo: 2; y = y_hi * 2 + y_lo), z: 12, core: 2. Of those that a mesh axis runs over, the one named last changes fastest.
Arguments:
- positions: float32 [48, 16, 8, 3, 16], P('gx', 'gy', 'gz'), may hold values from 0 to 5
- features: float32 [48, 16, 8, 16, 128], P('gx', 'gy', 'gz'), may hold values from -6 to 6
- species: int32 [48, 16, 8, 16], P('gx', 'gy', 'gz'), may hold values from 0 to 9
- counts: int32 [48, 16, 8], P('gx', 'gy', 'gz'), may hold values from 4 to 16
- species_energy: float32 [10], replicated, may hold values from -4 to 4
- radial_weight: float32 [8, 3, 128], replicated, may hold values from -2 to 2
- mix_weight: float32 [3, 128, 128], replicated, may hold values from -0.5 to 0.5
- readout: float32 [4, 128], replicated, may hold values from -0.5 to 0.5
Outputs:
- energies: float32 [48, 16, 8, 16], P('gx', 'gy', 'gz')
- forces: float32 [48, 16, 8, 3, 16], P('gx', 'gy', 'gz')
The draws below stay inside these ranges and needn't reach their ends.
All inputs are finite; a program needn't handle non-finite values.
Results may differ from the reference program's by a relative error of at most 0.0003.
Values sent between devices are 32-bit elements; how exact they have to be, the bound alone decides.
A program may use at most 64 MiB of HBM per device.

```python
import math
import jax
import jax.numpy as jnp
import numpy as np
from jax import lax

CH = 128
NB = 8
NSPEC = 10
CAP = 16
CX = 2
CY = 2
CZ = 2
NCX = 48
NCY = 16
NCZ = 8


def touch_ends(values, rng, smallest, high):
    longest = values.shape.index(max(values.shape))
    spots = []
    for shift in (0, 1):
        where = [jax.random.randint(jax.random.fold_in(rng, axis), (), 0, length) for axis, length in enumerate(values.shape)]
        where[longest] = (where[longest] + shift) % values.shape[longest]
        spots.append(tuple(where))
    return values.at[spots[0]].set(smallest).at[spots[1]].set(high)


def shard_levels(own_key, dims, shards, least, largest):
    factor_of, own = 1.0, jax.random.fold_in(own_key, 6)
    for position, shards_of in shards:
        heights = jnp.exp(jax.random.uniform(jax.random.fold_in(own, position), (shards_of,), jnp.float32, least / len(shards), largest / len(shards)))
        factor_of = factor_of * jnp.repeat(heights, dims[position] // shards_of).reshape([-1 if axis == position else 1 for axis in range(len(dims))])
    return factor_of


def noise(own_key, dims, scale, bound, shards=(), held_as=jnp.bfloat16):
    drawn = jax.random.normal(own_key, dims, jnp.float32) * scale
    if len(shards) > 0:
        drawn = shard_levels(own_key, dims, shards, -0.22, 0.18) * drawn
    return jnp.clip(drawn, min=-bound, max=bound).astype(held_as)


def setup_inputs(seed: int = 0) -> dict:
    splits = jax.random.split(jax.random.key(seed), 9)
    positions = jnp.clip(5.0 * jax.random.uniform(splits[0], (NCX, NCY, NCZ, 3, CAP), jnp.float32) ** shard_levels(splits[0], (NCX, NCY, NCZ, 3, CAP), ((0, 24), (1, 8), (2, 4)), -0.2, 0.2), 0.0, 5.0)
    features = noise(splits[1], (NCX, NCY, NCZ, CAP, CH), 1.0, 6.0, ((0, 24), (1, 8), (2, 4)), jnp.float32)
    species = touch_ends(jax.random.randint(splits[2], (NCX, NCY, NCZ, CAP), 0, NSPEC), jax.random.fold_in(splits[2], 1), 0, NSPEC - 1).astype(jnp.int32)
    counts = touch_ends(jax.random.randint(splits[3], (NCX, NCY, NCZ), CAP // 4, CAP + 1), jax.random.fold_in(splits[3], 1), CAP // 4, CAP).astype(jnp.int32)
    species_energy = noise(splits[4], (NSPEC,), 1.0, 4.0, (), jnp.float32)
    radial_weight = noise(splits[5], (NB, 3, CH), NB ** -0.5, 2.0, (), jnp.float32)
    mix_weight = noise(splits[6], (3, CH, CH), CH ** -0.5, 0.5, (), jnp.float32)
    readout = noise(splits[7], (4, CH), CH ** -0.5, 0.5, (), jnp.float32)
    return {"positions": positions, "features": features, "species": species, "counts": counts, "species_energy": species_energy, "radial_weight": radial_weight, "mix_weight": mix_weight, "readout": readout}


CUTOFF = 5.0
CELL_SIDE = 5.0
SOFTENING = 0.5
DEGREE_OF = np.array([0, 1, 1, 1, 2, 2, 2, 2, 2])
NEIGHBOUR_SHIFTS = np.array([[a, b, c] for a in (-1, 0, 1) for b in (-1, 0, 1) for c in (-1, 0, 1)]).T * CELL_SIDE

def harmonics(direction):
    xpart, ypart, zpart = (direction[0], direction[1], direction[2])
    root_three = math.sqrt(3.0)
    root_fifteen = math.sqrt(15.0)
    root_five = math.sqrt(5.0)
    square = xpart * xpart + ypart * ypart + zpart * zpart
    return jnp.stack([jnp.ones_like(xpart), root_three * xpart, root_three * ypart, root_three * zpart, root_fifteen * xpart * ypart, root_fifteen * ypart * zpart, 0.5 * root_five * (3.0 * zpart * zpart - square), root_fifteen * xpart * zpart, 0.5 * root_fifteen * (xpart * xpart - ypart * ypart)])

def cell_energy(ext_pos, ext_feat, corner, radial_weight, mix_weight, readout):
    slot_count = ext_pos.shape[-1]
    channels = ext_feat.shape[-1]
    basis_count = radial_weight.shape[0]
    highest = lax.Precision.HIGHEST
    anchor = jnp.zeros((), jnp.int32)
    block_pos = lax.dynamic_slice(ext_pos, (corner[0], corner[1], corner[2], anchor, anchor), (3, 3, 3, 3, slot_count))
    block_feat = lax.dynamic_slice(ext_feat, (corner[0], corner[1], corner[2], anchor, anchor), (3, 3, 3, slot_count, channels))
    own_pos = block_pos[1, 1, 1]
    offsets = jnp.asarray(NEIGHBOUR_SHIFTS, jnp.float32)
    near_pos = (jnp.transpose(block_pos.reshape(27, 3, slot_count), (1, 0, 2)) + offsets[:, :, None]).reshape(3, 27 * slot_count)
    near_feat = block_feat.reshape(27 * slot_count, channels)
    relative = near_pos[:, None, :] - own_pos[:, :, None]
    distance = jnp.sqrt(lax.optimization_barrier(jnp.sum(relative * relative, axis=0)) + SOFTENING * SOFTENING)
    direction = relative / distance
    scaled = distance / CUTOFF
    envelope = jnp.where(scaled < 1.0, 1.0 - 21.0 * scaled ** 5 + 35.0 * scaled ** 6 - 15.0 * scaled ** 7, 0.0)
    column = lax.broadcasted_iota(jnp.int32, (slot_count, 27 * slot_count), 1)
    row_ids = lax.broadcasted_iota(jnp.int32, (slot_count, 27 * slot_count), 0)
    keep_pair = jnp.where(column == row_ids + 13 * slot_count, 0.0, 1.0)
    weighting = envelope * keep_pair * math.sqrt(2.0 / CUTOFF) / distance
    orders = jnp.arange(1, basis_count + 1).astype(jnp.float32)
    radial = jnp.sin(orders[:, None, None] * (math.pi / CUTOFF) * distance[None]) * weighting[None]
    harmonic = harmonics(direction)
    pair_tiles = radial[:, None] * harmonic[None]
    moments = jnp.einsum('nmik,kc->inmc', pair_tiles, near_feat, precision=highest)
    radial_wide = radial_weight[:, DEGREE_OF, :]
    summed = lax.optimization_barrier(jnp.sum(moments * radial_wide[None], axis=1))
    scalar_inv = jnp.dot(summed[:, 0], mix_weight[0], precision=highest)
    vector_part = jnp.einsum('imc,cd->imd', summed[:, 1:4], mix_weight[1], precision=highest)
    tensor_part = jnp.einsum('imc,cd->imd', summed[:, 4:9], mix_weight[2], precision=highest)
    vector_inv = lax.optimization_barrier(jnp.sum(vector_part * vector_part, axis=1))
    tensor_inv = lax.optimization_barrier(jnp.sum(tensor_part * tensor_part, axis=1))
    return jnp.dot(scalar_inv, readout[0], precision=highest) + jnp.dot(vector_inv, readout[1], precision=highest) + jnp.dot(tensor_inv, readout[2], precision=highest) + jnp.dot(scalar_inv * vector_inv, readout[3], precision=highest)

def grid_energies(ext_pos, ext_feat, cells_x, cells_y, cells_z, group_size, radial_weight, mix_weight, readout):
    cell_count = cells_x * cells_y * cells_z
    cell_ids = jnp.arange(cell_count, dtype=jnp.int32).reshape(cell_count // group_size, group_size)

    def one_cell(number):
        corner = jnp.stack([number // (cells_y * cells_z), number // cells_z % cells_y, number % cells_z]).astype(jnp.int32)
        return cell_energy(ext_pos, ext_feat, corner, radial_weight, mix_weight, readout)

    def per_group(id_row):
        return jax.vmap(one_cell)(id_row)
    result = lax.map(jax.checkpoint(per_group), cell_ids)
    return result.reshape(cells_x, cells_y, cells_z, ext_pos.shape[-1])

def reference(positions, features, species, counts, species_energy, radial_weight, mix_weight, readout):
    slot_count = positions.shape[-1]
    occupied = (jnp.arange(slot_count, dtype=jnp.int32)[None, None, None, :] < counts[..., None]).astype(jnp.float32)
    masked = features * occupied[..., None]
    wrap_pad = ((1, 1), (1, 1), (1, 1), (0, 0), (0, 0))
    ext_feat = jnp.pad(masked, wrap_pad, mode='wrap')

    def energy_sum(pos):
        ext_pos = jnp.pad(pos, wrap_pad, mode='wrap')
        layer = grid_energies(ext_pos, ext_feat, NCX, NCY, NCZ, CX * CY * CZ, radial_weight, mix_weight, readout)
        return (jnp.sum(layer * occupied), layer)
    (summed_energy, layer), gradient = jax.value_and_grad(energy_sum, has_aux=True)(positions)
    species_hot = (species[..., None] == jnp.arange(species_energy.shape[0], dtype=jnp.int32)).astype(jnp.float32)
    table_part = lax.optimization_barrier(jnp.sum(species_hot * species_energy, axis=-1))
    energies = occupied * (layer + table_part)
    return (energies, -gradient)
```

```python
import math

import jax
import jax.numpy as jnp
import numpy as np
from jax import lax
from jax.experimental import pallas as pl
from jax.experimental.pallas import tpu as pltpu
from jax.sharding import PartitionSpec as P

CUTOFF = 5.0
CELL_SIDE = 5.0
SOFTENING = 0.5
BASIS = 8
SLOTS = 16
LANES = 128
CHUNKS = 4
NEAR = CHUNKS * LANES
ROWS = BASIS * 9 * SLOTS
DEGREE_OF = (0, 1, 1, 1, 2, 2, 2, 2, 2)
SELF = 13
MESH = pl.DeviceIdType.MESH
AXES = ("gx", "gy", "gz")
R3, R5, R15 = math.sqrt(3.0), math.sqrt(5.0), math.sqrt(15.0)
F32, BF16 = jnp.float32, jnp.bfloat16

OFFSETS = [(a, b, c) for a in (-1, 0, 1) for b in (-1, 0, 1) for c in (-1, 0, 1)]
CELLS = [(x, y, z) for x in (0, 1) for y in (0, 1) for z in (0, 1)]


def near_table(cell):
    sign = [1 if c == 1 else -1 for c in cell]
    rim = [0 if s == 1 else 1 for s in sign]
    taken = {(0, q) for q in range(8)}
    table = [(0, q, SELF, q) for q in range(8)]
    late = []
    for size in (1, 2, 3):
        for subset in range(1, 8):
            dims = [d for d in range(3) if subset >> d & 1]
            if len(dims) != size:
                continue
            off = [sign[d] if d in dims else 0 for d in range(3)]
            domain = OFFSETS.index(tuple(off))
            for q, coords in enumerate(CELLS):
                if any(coords[d] != rim[d] for d in dims):
                    continue
                for chunk in range(1, CHUNKS):
                    if (chunk, q) not in taken:
                        taken.add((chunk, q))
                        table.append((chunk, q, domain, q))
                        break
                else:
                    late.append((domain, q))
    for domain, q in late:
        chunk, place = min(
            (c, p) for c in range(1, CHUNKS) for p in range(8) if (c, p) not in taken
        )
        taken.add((chunk, place))
        table.append((chunk, place, domain, q))
    return table


TABLES = [near_table(cell) for cell in CELLS]


def grouped(table, chunk):
    groups = {}
    for c, place, domain, q in table:
        if c == chunk:
            groups.setdefault((domain, (place - q) % 8), []).append(place)
    return sorted(groups.items())


def places_mask(places):
    lane = lax.broadcasted_iota(jnp.int32, (8, LANES), 1)
    mask = None
    for place in places:
        one = (lane >= place * SLOTS) & (lane < (place + 1) * SLOTS)
        mask = one if mask is None else mask | one
    return mask


def neighbour(domain):
    place = []
    for axis, step in zip(AXES, OFFSETS[domain]):
        count = lax.axis_size(axis)
        place.append(lax.rem(lax.axis_index(axis) + step + count, count))
    return tuple(place)


def rim_of(domain):
    return tuple(
        pl.ds(0, 2) if step == 0 else pl.ds(1 if step == 1 else 0, 1) for step in OFFSETS[domain]
    )


def greet():
    barrier = pltpu.get_barrier_semaphore()
    for domain in range(27):
        if domain != SELF:
            pl.semaphore_signal(
                barrier, inc=1, device_id=neighbour(domain), device_id_type=MESH
            )
    return barrier


def halo_kernel(pos_ref, feat_ref, counts_ref, tiles_ref, feats_ref, tile, masked, sends, recvs, own):
    barrier = greet()
    slot = lax.broadcasted_iota(jnp.int32, (SLOTS, LANES), 0)
    tile[...] = jnp.zeros_like(tile)
    for q, (x, y, z) in enumerate(CELLS):
        tile[0:3, q * SLOTS : (q + 1) * SLOTS] = pos_ref[x, y, :, z, :]
        masked[x, y, z] = jnp.where(slot < counts_ref[x, y, z], feat_ref[x, y, z], 0.0)
    lane = lax.broadcasted_iota(jnp.int32, (8, LANES), 1)
    row = lax.broadcasted_iota(jnp.int32, (8, LANES), 0)
    shift = jnp.where(row == 0, lane // 64, jnp.where(row == 1, lane // 32 % 2, lane // 16 % 2))
    tile[...] = tile[...] + CELL_SIDE * shift.astype(F32)
    pl.semaphore_wait(barrier, 26)
    mine = [
        pltpu.make_async_copy(tile, tiles_ref.at[SELF], own.at[0]),
        pltpu.make_async_copy(masked, feats_ref.at[SELF], own.at[1]),
    ]
    copies = []
    for domain in range(27):
        if domain == SELF:
            continue
        there, rim, back = neighbour(domain), rim_of(domain), 26 - domain
        copies.append(
            pltpu.make_async_remote_copy(
                tile, tiles_ref.at[back], sends.at[0, domain], recvs.at[0, back],
                device_id=there, device_id_type=MESH,
            )
        )
        copies.append(
            pltpu.make_async_remote_copy(
                masked.at[rim], feats_ref.at[(back,) + rim], sends.at[1, domain],
                recvs.at[1, back], device_id=there, device_id_type=MESH,
            )
        )
    for copy in copies:
        copy.start()
    for copy in mine:
        copy.start()
    for copy in mine:
        copy.wait()
    for copy in copies:
        copy.wait()


def halves(value):
    high = value.astype(BF16)
    return high, (value - high.astype(F32)).astype(BF16)


def dot(a, b, rhs_dim=0):
    return lax.dot_general(
        a, b, (((1,), (rhs_dim,)), ((), ())), preferred_element_type=F32
    )


def dot_split(a, b, rhs_dim=0):
    a_high, a_low = halves(a)
    b_high, b_low = halves(b)
    return (
        dot(a_low, b_high, rhs_dim) + dot(a_high, b_low, rhs_dim) + dot(a_high, b_high, rhs_dim)
    )


def harmonics(ux, uy, uz):
    square = ux * ux + uy * uy + uz * uz
    return [
        None,
        R3 * ux,
        R3 * uy,
        R3 * uz,
        R15 * ux * uy,
        R15 * uy * uz,
        0.5 * R5 * (3.0 * uz * uz - square),
        R15 * ux * uz,
        0.5 * R15 * (ux * ux - uy * uy),
    ]


def radial_parts(distance, inverse, keep):
    t = jnp.minimum(distance * (1.0 / CUTOFF), 1.0)
    phi = math.pi * (t - 0.5)
    sq = phi * phi
    sine, cosine = 0.0, 0.0
    for k in range(6, -1, -1):
        if k < 6:
            sine = sine * sq + (-1) ** k / math.factorial(2 * k + 1)
        cosine = cosine * sq + (-1) ** k / math.factorial(2 * k)
    s1, c1 = cosine, -(sine * phi)
    t2 = t * t
    t4 = t2 * t2
    env = jnp.where(keep, 1.0 + t4 * t * (-21.0 + t * (35.0 - 15.0 * t)), 0.0)
    gap = 1.0 - t
    env_d = jnp.where(keep, (-105.0 / CUTOFF) * t4 * gap * gap, 0.0)
    scale = math.sqrt(2.0 / CUTOFF)
    w = scale * env * inverse
    w_d = inverse * (scale * env_d - w)
    twice = 2.0 * c1
    sines, cosines = [s1], [c1]
    for n in range(1, BASIS):
        sines.append(twice * sines[-1] - (sines[-2] if n > 1 else 0.0))
        cosines.append(twice * cosines[-1] - (cosines[-2] if n > 1 else 1.0))
    values = [s * w for s in sines]
    slopes = [
        ((n + 1) * math.pi / CUTOFF) * (c * w) + s * w_d
        for n, (s, c) in enumerate(zip(sines, cosines))
    ]
    return values, slopes


def force_kernel(
    tiles_ref, feats_ref, species_ref, counts_ref, table_ref, radial_ref, mix_ref, readout_ref,
    energy_ref, grads_ref,
    npos, post, fcat, fback, pair, mom, summed, rad, geo, gpair, dpair, ngrad, center,
):
    row = lax.broadcasted_iota(jnp.int32, (8, LANES), 0)
    for s in range(8):
        for chunk in range(CHUNKS):
            value = jnp.full((8, LANES), 100.0, F32)
            for (domain, turn), places in grouped(TABLES[s], chunk):
                ox, oy, oz = (2.0 * CELL_SIDE * o for o in OFFSETS[domain])
                piece = tiles_ref[domain]
                if domain != SELF:
                    piece = piece + jnp.where(row == 0, ox, jnp.where(row == 1, oy, oz))
                if turn:
                    piece = pltpu.roll(piece, turn * SLOTS, 1)
                value = piece if len(places) == 8 else jnp.where(places_mask(places), piece, value)
            npos[s, :, chunk * LANES : (chunk + 1) * LANES] = value
        filled = {(c, p): (domain, q) for c, p, domain, q in TABLES[s]}
        for chunk in range(CHUNKS):
            for place in range(8):
                at = slice(chunk * LANES + place * SLOTS, chunk * LANES + (place + 1) * SLOTS)
                low_at = slice(NEAR + at.start, NEAR + at.stop)
                if (chunk, place) in filled:
                    domain, q = filled[(chunk, place)]
                    high, low = halves(feats_ref[domain * 8 + q])
                else:
                    high = low = jnp.zeros((SLOTS, LANES), BF16)
                fcat[s, at, 0:128] = high
                fcat[s, at, 128:256] = low
                fcat[s, low_at, 0:128] = high
                fcat[s, low_at, 128:256] = jnp.zeros((SLOTS, LANES), BF16)
                fback[s, at, 0:128] = high
                fback[s, at, 128:256] = high
                fback[s, at, 256:384] = low
    mine = tiles_ref[SELF]
    post[...] = jnp.transpose(jnp.concatenate([mine] * 16, axis=0))
    ngrad[...] = jnp.zeros_like(ngrad)

    def forward(s, carry):
        own = pl.ds(pl.multiple_of(s * SLOTS, SLOTS), SLOTS)
        for chunk in range(CHUNKS):
            at = slice(chunk * LANES, (chunk + 1) * LANES)
            low_at = slice(NEAR + at.start, NEAR + at.stop)
            rx, ry, rz = (npos[s, a : a + 1, at] - post[own, a : a + 1] for a in range(3))
            squared = rx * rx + ry * ry + rz * rz + SOFTENING * SOFTENING
            inverse = lax.rsqrt(squared)
            distance = squared * inverse
            keep = distance < CUTOFF
            if chunk == 0:
                lane = lax.broadcasted_iota(jnp.int32, (SLOTS, LANES), 1)
                slot = lax.broadcasted_iota(jnp.int32, (SLOTS, LANES), 0)
                keep = keep & (lane != slot + s * SLOTS)
            values, slopes = radial_parts(distance, inverse, keep)
            ux, uy, uz = rx * inverse, ry * inverse, rz * inverse
            for a, part in enumerate((ux, uy, uz, inverse)):
                geo[s, a, :, at] = part
            harmonic = harmonics(ux, uy, uz)
            for n in range(BASIS):
                rad[s, n, :, at] = values[n]
                rad[s, BASIS + n, :, at] = slopes[n]
                for m in range(9):
                    value = values[n] if m == 0 else values[n] * harmonic[m]
                    high, low = halves(value)
                    rows = slice((n * 9 + m) * SLOTS, (n * 9 + m + 1) * SLOTS)
                    pair[rows, at] = high
                    pair[rows, low_at] = low
        mom[...] = dot(pair[...], fcat[s])
        for m in range(9):
            total = None
            for n in range(BASIS):
                rows = slice((n * 9 + m) * SLOTS, (n * 9 + m + 1) * SLOTS)
                l = DEGREE_OF[m]
                term = (mom[rows, 0:128] + mom[rows, 128:256]) * radial_ref[l, n : n + 1, :]
                total = term if total is None else total + term
            summed[m, own, :] = total
        return carry

    lax.fori_loop(0, 8, forward, 0)

    slot = lax.broadcasted_iota(jnp.int32, (SLOTS, LANES), 0)
    occupied = jnp.concatenate(
        [jnp.where(slot < counts_ref[x, y, z], 1.0, 0.0) for x, y, z in CELLS], axis=0
    )
    mixed = []
    for l, span in enumerate((slice(0, 1), slice(1, 4), slice(4, 9))):
        part = summed[span].reshape((span.stop - span.start) * LANES, LANES)
        part = dot_split(part, mix_ref[l])
        mixed += [part[i * LANES : (i + 1) * LANES] for i in range(span.stop - span.start)]
    q0 = mixed[0]
    q1 = sum(v * v for v in mixed[1:4])
    q2 = sum(v * v for v in mixed[4:9])
    r0, r1, r2, r3 = (readout_ref[i : i + 1, :] for i in range(4))
    layer = q0 * r0 + q1 * r1 + q2 * r2 + (q0 * q1) * r3
    layer = jnp.sum(jnp.transpose(layer), axis=0, keepdims=True)
    lane16 = lax.broadcasted_iota(jnp.int32, (1, SLOTS), 1)
    for q, (x, y, z) in enumerate(CELLS):
        kind = species_ref[x, y, z : z + 1, :]
        value = layer[:, q * SLOTS : (q + 1) * SLOTS]
        for k in range(table_ref.shape[0]):
            value = value + jnp.where(kind == k, table_ref[k], 0.0)
        energy_ref[x, y, z : z + 1, :] = jnp.where(lane16 < counts_ref[x, y, z], value, 0.0)
    slope1 = 2.0 * occupied * (r1 + q0 * r3)
    slope2 = 2.0 * occupied * r2
    back = [occupied * (r0 + q1 * r3)]
    back += [v * slope1 for v in mixed[1:4]]
    back += [v * slope2 for v in mixed[4:9]]
    for l, span in enumerate((slice(0, 1), slice(1, 4), slice(4, 9))):
        part = dot_split(jnp.concatenate(back[span], axis=0), mix_ref[l], 1)
        summed[span] = part.reshape(span.stop - span.start, LANES, LANES)

    def backward(s, carry):
        own = pl.ds(pl.multiple_of(s * SLOTS, SLOTS), SLOTS)
        for m in range(9):
            slope = summed[m, own, :]
            l = DEGREE_OF[m]
            for n in range(BASIS):
                rows = slice((n * 9 + m) * SLOTS, (n * 9 + m + 1) * SLOTS)
                high, low = halves(slope * radial_ref[l, n : n + 1, :])
                gpair[rows, 0:128] = high
                gpair[rows, 128:256] = low
                gpair[rows, 256:384] = high
        dpair[...] = dot(gpair[...], fback[s], 1)
        pull = [None] * 3
        for chunk in range(CHUNKS):
            at = slice(chunk * LANES, (chunk + 1) * LANES)
            ux, uy, uz, inverse = (geo[s, a, :, at] for a in range(4))
            harmonic = harmonics(ux, uy, uz)
            amp = [None] * 9
            along = None
            for n in range(BASIS):
                value, slope = rad[s, n, :, at], rad[s, BASIS + n, :, at]
                inner = None
                for m in range(9):
                    part = dpair[(n * 9 + m) * SLOTS : (n * 9 + m + 1) * SLOTS, at]
                    if m > 0:
                        amp[m] = part * value if n == 0 else amp[m] + part * value
                    inner = part if m == 0 else inner + part * harmonic[m]
                along = inner * slope if n == 0 else along + inner * slope
            vx = R3 * amp[1] + R15 * (uy * amp[4] + uz * amp[7] + ux * amp[8]) - R5 * (ux * amp[6])
            vy = R3 * amp[2] + R15 * (ux * amp[4] + uz * amp[5] - uy * amp[8]) - R5 * (uy * amp[6])
            vz = R3 * amp[3] + R15 * (uy * amp[5] + ux * amp[7]) + (2.0 * R5) * (uz * amp[6])
            radial = along - inverse * (ux * vx + uy * vy + uz * vz)
            for a, (u, v) in enumerate(((ux, vx), (uy, vy), (uz, vz))):
                slope = u * radial + inverse * v
                ngrad[s, a : a + 1, at] = jnp.sum(slope, axis=0, keepdims=True)
                pull[a] = slope if chunk == 0 else pull[a] + slope
        for a in range(3):
            center[a, own, :] = pull[a]
        return carry

    lax.fori_loop(0, 8, backward, 0)

    grads_ref[...] = jnp.zeros_like(grads_ref)
    for a in range(3):
        grads_ref[SELF, a : a + 1, :] = -jnp.sum(jnp.transpose(center[a]), axis=0, keepdims=True)
    for s in range(8):
        for chunk in range(CHUNKS):
            whole = ngrad[s, :, chunk * LANES : (chunk + 1) * LANES]
            for (domain, turn), places in grouped(TABLES[s], chunk):
                piece = whole if len(places) == 8 else jnp.where(places_mask(places), whole, 0.0)
                if turn:
                    piece = pltpu.roll(piece, (8 - turn) * SLOTS, 1)
                grads_ref[domain] = grads_ref[domain] + piece


def return_kernel(grads_ref, force_ref, landed, sends, recvs):
    barrier = greet()
    pl.semaphore_wait(barrier, 26)
    copies = []
    for domain in range(27):
        if domain != SELF:
            copies.append(
                pltpu.make_async_remote_copy(
                    grads_ref.at[domain], landed.at[26 - domain], sends.at[domain],
                    recvs.at[26 - domain], device_id=neighbour(domain), device_id_type=MESH,
                )
            )
    for copy in copies:
        copy.start()
    for copy in copies:
        copy.wait()
    total = grads_ref[SELF]
    for domain in range(27):
        if domain != SELF:
            total = total + landed[domain]
    total = -total
    for q, (x, y, z) in enumerate(CELLS):
        force_ref[x, y, :, z, :] = total[0:3, q * SLOTS : (q + 1) * SLOTS]


VMEM = pl.BlockSpec(memory_space=pltpu.VMEM)
SMEM = pl.BlockSpec(memory_space=pltpu.SMEM)
ANY = pl.BlockSpec(memory_space=pl.ANY)


def halo(positions, features, counts):
    return pl.pallas_call(
        halo_kernel,
        out_shape=(
            jax.ShapeDtypeStruct((27, 8, LANES), F32),
            jax.ShapeDtypeStruct((27, 2, 2, 2, SLOTS, LANES), F32),
        ),
        in_specs=[VMEM, VMEM, SMEM],
        out_specs=(ANY, ANY),
        scratch_shapes=[
            pltpu.VMEM((8, LANES), F32),
            pltpu.VMEM((2, 2, 2, SLOTS, LANES), F32),
            pltpu.SemaphoreType.DMA((2, 27)),
            pltpu.SemaphoreType.DMA((2, 27)),
            pltpu.SemaphoreType.DMA((2,)),
        ],
        compiler_params=pltpu.CompilerParams(collective_id=0, has_side_effects=True),
    )(positions, features, counts)


def cell_forces(tiles, feats, species, counts, table, radial, mix, readout):
    return pl.pallas_call(
        force_kernel,
        out_shape=(
            jax.ShapeDtypeStruct((2, 2, 2, SLOTS), F32),
            jax.ShapeDtypeStruct((27, 8, LANES), F32),
        ),
        in_specs=[VMEM, VMEM, VMEM, SMEM, SMEM, VMEM, VMEM, VMEM],
        out_specs=(VMEM, VMEM),
        scratch_shapes=[
            pltpu.VMEM((8, 8, NEAR), F32),
            pltpu.VMEM((LANES, LANES), F32),
            pltpu.VMEM((8, 2 * NEAR, 256), BF16),
            pltpu.VMEM((8, NEAR, 384), BF16),
            pltpu.VMEM((ROWS, 2 * NEAR), BF16),
            pltpu.VMEM((ROWS, 256), F32),
            pltpu.VMEM((9, LANES, LANES), F32),
            pltpu.VMEM((8, 2 * BASIS, SLOTS, NEAR), F32),
            pltpu.VMEM((8, 4, SLOTS, NEAR), F32),
            pltpu.VMEM((ROWS, 384), BF16),
            pltpu.VMEM((ROWS, NEAR), F32),
            pltpu.VMEM((8, 8, NEAR), F32),
            pltpu.VMEM((3, LANES, LANES), F32),
        ],
        compiler_params=pltpu.CompilerParams(vmem_limit_bytes=48 * 2**20),
    )(tiles, feats, species, counts, table, radial, mix, readout)


def give_back(grads):
    return pl.pallas_call(
        return_kernel,
        out_shape=jax.ShapeDtypeStruct((2, 2, 3, 2, SLOTS), F32),
        in_specs=[VMEM],
        out_specs=VMEM,
        scratch_shapes=[
            pltpu.VMEM((27, 8, LANES), F32),
            pltpu.SemaphoreType.DMA((27,)),
            pltpu.SemaphoreType.DMA((27,)),
        ],
        compiler_params=pltpu.CompilerParams(collective_id=1, has_side_effects=True),
    )(grads)


def per_device(positions, features, species, counts, species_energy, radial_weight, mix_weight, readout):
    tiles, feats = halo(jnp.swapaxes(positions, 2, 3), features, counts)
    feats = feats.reshape(27 * 8, SLOTS, LANES)
    energies, grads = cell_forces(
        tiles, feats, species, counts, species_energy, jnp.swapaxes(radial_weight, 0, 1),
        mix_weight, readout,
    )
    return energies, jnp.swapaxes(give_back(grads), 2, 3)


def solution(mesh):
    grid = P("gx", "gy", "gz")
    return jax.shard_map(
        per_device,
        mesh=mesh,
        in_specs=(grid, grid, grid, grid, P(), P(), P(), P()),
        out_specs=(grid, grid),
        check_vma=False,
    )
```

```python
import math

import jax
import jax.numpy as jnp
import numpy as np
from jax import lax
from jax.experimental import pallas as pl
from jax.experimental.pallas import tpu as pltpu
from jax.sharding import PartitionSpec as P

CUTOFF = 5.0
CELL_SIDE = 5.0
SOFTENING = 0.5
BASIS = 8
SLOTS = 16
LANES = 128
CHUNKS = 4
NEAR = CHUNKS * LANES
GHOST = NEAR - LANES
ROWS = BASIS * 9 * SLOTS
DEGREE_OF = (0, 1, 1, 1, 2, 2, 2, 2, 2)
SELF = 13
MESH = pl.DeviceIdType.MESH
AXES = ("gx", "gy", "gz")
R3, R5, R15 = math.sqrt(3.0), math.sqrt(5.0), math.sqrt(15.0)
F32, BF16 = jnp.float32, jnp.bfloat16

OFFSETS = [(a, b, c) for a in (-1, 0, 1) for b in (-1, 0, 1) for c in (-1, 0, 1)]
CELLS = [(x, y, z) for x in (0, 1) for y in (0, 1) for z in (0, 1)]


def near_table(cell):
    sign = [1 if c == 1 else -1 for c in cell]
    rim = [0 if s == 1 else 1 for s in sign]
    taken = {(0, q) for q in range(8)}
    table = [(0, q, SELF, q) for q in range(8)]
    late = []
    for size in (1, 2, 3):
        for subset in range(1, 8):
            dims = [d for d in range(3) if subset >> d & 1]
            if len(dims) != size:
                continue
            off = [sign[d] if d in dims else 0 for d in range(3)]
            domain = OFFSETS.index(tuple(off))
            for q, coords in enumerate(CELLS):
                if any(coords[d] != rim[d] for d in dims):
                    continue
                for chunk in range(1, CHUNKS):
                    if (chunk, q) not in taken:
                        taken.add((chunk, q))
                        table.append((chunk, q, domain, q))
                        break
                else:
                    late.append((domain, q))
    for domain, q in late:
        chunk, place = min(
            (c, p) for c in range(1, CHUNKS) for p in range(8) if (c, p) not in taken
        )
        taken.add((chunk, place))
        table.append((chunk, place, domain, q))
    return table


TABLES = [near_table(cell) for cell in CELLS]


def grouped(table, chunk):
    groups = {}
    for c, place, domain, q in table:
        if c == chunk:
            groups.setdefault((domain, (place - q) % 8), []).append(place)
    return sorted(groups.items())


def places_mask(places):
    lane = lax.broadcasted_iota(jnp.int32, (8, LANES), 1)
    mask = None
    for place in places:
        one = (lane >= place * SLOTS) & (lane < (place + 1) * SLOTS)
        mask = one if mask is None else mask | one
    return mask


def neighbour(domain):
    place = []
    for axis, step in zip(AXES, OFFSETS[domain]):
        count = lax.axis_size(axis)
        place.append(lax.rem(lax.axis_index(axis) + step + count, count))
    return tuple(place)


def rim_of(domain):
    return tuple(
        pl.ds(0, 2) if step == 0 else pl.ds(1 if step == 1 else 0, 1) for step in OFFSETS[domain]
    )


def greet():
    barrier = pltpu.get_barrier_semaphore()
    for domain in range(27):
        if domain != SELF:
            pl.semaphore_signal(
                barrier, inc=1, device_id=neighbour(domain), device_id_type=MESH
            )
    return barrier


def halves(value):
    high = value.astype(BF16)
    return high, (value - high.astype(F32)).astype(BF16)


def dot(a, b, rhs_dim=0):
    return lax.dot_general(
        a, b, (((1,), (rhs_dim,)), ((), ())), preferred_element_type=F32
    )


def dot_split(a, b, rhs_dim=0):
    a_high, a_low = halves(a)
    b_high, b_low = halves(b)
    return (
        dot(a_low, b_high, rhs_dim) + dot(a_high, b_low, rhs_dim) + dot(a_high, b_high, rhs_dim)
    )


def harmonics(ux, uy, uz):
    square = ux * ux + uy * uy + uz * uz
    return [
        None,
        R3 * ux,
        R3 * uy,
        R3 * uz,
        R15 * ux * uy,
        R15 * uy * uz,
        0.5 * R5 * (3.0 * uz * uz - square),
        R15 * ux * uz,
        0.5 * R15 * (ux * ux - uy * uy),
    ]


def radial_parts(distance, inverse, keep):
    t = jnp.minimum(distance * (1.0 / CUTOFF), 1.0)
    phi = math.pi * (t - 0.5)
    sq = phi * phi
    sine, cosine = 0.0, 0.0
    for k in range(6, -1, -1):
        if k < 6:
            sine = sine * sq + (-1) ** k / math.factorial(2 * k + 1)
        cosine = cosine * sq + (-1) ** k / math.factorial(2 * k)
    s1, c1 = cosine, -(sine * phi)
    t2 = t * t
    t4 = t2 * t2
    env = jnp.where(keep, 1.0 + t4 * t * (-21.0 + t * (35.0 - 15.0 * t)), 0.0)
    gap = 1.0 - t
    env_d = jnp.where(keep, (-105.0 / CUTOFF) * t4 * gap * gap, 0.0)
    scale = math.sqrt(2.0 / CUTOFF)
    w = scale * env * inverse
    w_d = inverse * (scale * env_d - w)
    twice = 2.0 * c1
    sines, cosines = [s1], [c1]
    for n in range(1, BASIS):
        sines.append(twice * sines[-1] - (sines[-2] if n > 1 else 0.0))
        cosines.append(twice * cosines[-1] - (cosines[-2] if n > 1 else 1.0))
    values = [s * w for s in sines]
    slopes = [
        ((n + 1) * math.pi / CUTOFF) * (c * w) + s * w_d
        for n, (s, c) in enumerate(zip(sines, cosines))
    ]
    return values, slopes


def near_pairs(s, chunk, npos, post, geo, rad, pair, high_at, low_at):
    own = pl.ds(pl.multiple_of(s * SLOTS, SLOTS), SLOTS)
    at = slice(chunk * LANES, (chunk + 1) * LANES)
    rx, ry, rz = (npos[s, a : a + 1, at] - post[own, a : a + 1] for a in range(3))
    squared = rx * rx + ry * ry + rz * rz + SOFTENING * SOFTENING
    inverse = lax.rsqrt(squared)
    distance = squared * inverse
    keep = distance < CUTOFF
    if chunk == 0:
        lane = lax.broadcasted_iota(jnp.int32, (SLOTS, LANES), 1)
        slot = lax.broadcasted_iota(jnp.int32, (SLOTS, LANES), 0)
        keep = keep & (lane != slot + s * SLOTS)
    values, slopes = radial_parts(distance, inverse, keep)
    ux, uy, uz = rx * inverse, ry * inverse, rz * inverse
    for a, part in enumerate((ux, uy, uz, inverse)):
        geo[s, a, :, at] = part
    harmonic = harmonics(ux, uy, uz)
    for n in range(BASIS):
        rad[s, n, :, at] = values[n]
        rad[s, BASIS + n, :, at] = slopes[n]
        for m in range(9):
            high, low = halves(values[n] if m == 0 else values[n] * harmonic[m])
            rows = slice((n * 9 + m) * SLOTS, (n * 9 + m + 1) * SLOTS)
            pair[rows, high_at : high_at + LANES] = high
            pair[rows, low_at : low_at + LANES] = low


def weighted(mom, radial, m):
    total = None
    for n in range(BASIS):
        rows = slice((n * 9 + m) * SLOTS, (n * 9 + m + 1) * SLOTS)
        l = DEGREE_OF[m]
        term = (mom[rows, 0:128] + mom[rows, 128:256]) * radial[l, n : n + 1, :]
        total = term if total is None else total + term
    return total


def put_near(s, chunk, npos, tiles):
    row = lax.broadcasted_iota(jnp.int32, (8, LANES), 0)
    value = jnp.full((8, LANES), 100.0, F32)
    for (domain, turn), places in grouped(TABLES[s], chunk):
        ox, oy, oz = (2.0 * CELL_SIDE * o for o in OFFSETS[domain])
        piece = tiles[domain]
        if domain != SELF:
            piece = piece + jnp.where(row == 0, ox, jnp.where(row == 1, oy, oz))
        if turn:
            piece = pltpu.roll(piece, turn * SLOTS, 1)
        value = piece if len(places) == 8 else jnp.where(places_mask(places), piece, value)
    npos[s, :, chunk * LANES : (chunk + 1) * LANES] = value


def put_features(high, low, fcat, s, at, low_by, fback, back_at):
    rows, low_rows = slice(at, at + SLOTS), slice(at + low_by, at + low_by + SLOTS)
    where = () if s is None else (s,)
    fcat[where + (rows, slice(0, 128))] = high
    fcat[where + (rows, slice(128, 256))] = low
    fcat[where + (low_rows, slice(0, 128))] = high
    fcat[where + (low_rows, slice(128, 256))] = jnp.zeros_like(low)
    for b in range(8) if s is None else (s,):
        rows = slice(back_at, back_at + SLOTS)
        fback[b, rows, 0:128] = high
        fback[b, rows, 128:256] = high
        fback[b, rows, 256:384] = low


def whole_kernel(
    pos_hbm, feat_hbm, species_hbm, counts_hbm, table_hbm, radial_hbm, mix_hbm, readout_hbm,
    energy_ref, force_ref,
    pos, feat, species, counts, table, radial, mix, readout, loads,
    tiles, feats, sends, recvs, landed, back_sends, back_recvs,
    npos, post, fown, fcat, fback, opair, pair, mom, summed, rad, geo, gpair, dpair, ngrad, center,
    grads,
):
    barrier = greet()
    held = [
        pltpu.make_async_copy(source, target, loads.at[i])
        for i, (source, target) in enumerate(
            (
                (pos_hbm, pos), (counts_hbm, counts), (feat_hbm, feat), (radial_hbm, radial),
                (mix_hbm, mix), (readout_hbm, readout), (species_hbm, species), (table_hbm, table),
            )
        )
    ]
    for copy in held:
        copy.start()
    slot = lax.broadcasted_iota(jnp.int32, (SLOTS, LANES), 0)
    tiles[SELF] = jnp.zeros((8, LANES), F32)
    ngrad[...] = jnp.zeros_like(ngrad)
    grads[...] = jnp.zeros_like(grads)
    for copy in held[:3]:
        copy.wait()
    for q, (x, y, z) in enumerate(CELLS):
        tiles[SELF, 0:3, q * SLOTS : (q + 1) * SLOTS] = pos[x, y, :, z, :]
        occupied = slot < counts[x, y : y + 1, z : z + 1]
        feats[SELF, x, y, z] = jnp.where(occupied, feat[x, y, z], 0.0)
    lane = lax.broadcasted_iota(jnp.int32, (8, LANES), 1)
    row = lax.broadcasted_iota(jnp.int32, (8, LANES), 0)
    shift = jnp.where(row == 0, lane // 64, jnp.where(row == 1, lane // 32 % 2, lane // 16 % 2))
    tiles[SELF] = tiles[SELF] + CELL_SIDE * shift.astype(F32)

    copies = []
    for domain in range(27):
        if domain == SELF:
            continue
        there, rim, back = neighbour(domain), rim_of(domain), 26 - domain
        copies.append(
            pltpu.make_async_remote_copy(
                tiles.at[SELF], tiles.at[back], sends.at[0, domain], recvs.at[0, back],
                device_id=there, device_id_type=MESH,
            )
        )
        copies.append(
            pltpu.make_async_remote_copy(
                feats.at[(SELF,) + rim], feats.at[(back,) + rim], sends.at[1, domain],
                recvs.at[1, back], device_id=there, device_id_type=MESH,
            )
        )
    pl.semaphore_wait(barrier, 26)
    for copy in copies:
        copy.start()

    for s in range(8):
        put_near(s, 0, npos, tiles)
    mine = tiles[SELF]
    post[...] = jnp.transpose(jnp.concatenate([mine] * 16, axis=0))
    for q, (x, y, z) in enumerate(CELLS):
        high, low = halves(feats[SELF, x, y, z])
        put_features(high, low, fown, None, q * SLOTS, LANES, fback, q * SLOTS)
    for copy in held[3:]:
        copy.wait()

    def inside(s, carry):
        near_pairs(s, 0, npos, post, geo, rad, opair, 0, LANES)
        mom[...] = dot(opair[...], fown[...])
        own = pl.ds(pl.multiple_of(s * SLOTS, SLOTS), SLOTS)
        for m in range(9):
            summed[m, own, :] = weighted(mom, radial, m)
        return carry

    lax.fori_loop(0, 8, inside, 0)

    for copy in copies:
        copy.wait()
    for s in range(8):
        for chunk in range(1, CHUNKS):
            put_near(s, chunk, npos, tiles)
        filled = {(c, p): (domain, q) for c, p, domain, q in TABLES[s]}
        for chunk in range(1, CHUNKS):
            for place in range(8):
                at = (chunk - 1) * LANES + place * SLOTS
                if (chunk, place) in filled:
                    domain, q = filled[(chunk, place)]
                    high, low = halves(feats[(domain,) + CELLS[q]])
                else:
                    high = low = jnp.zeros((SLOTS, LANES), BF16)
                put_features(high, low, fcat, s, at, GHOST, fback, at + LANES)

    def outside(s, carry):
        for chunk in range(1, CHUNKS):
            at = (chunk - 1) * LANES
            near_pairs(s, chunk, npos, post, geo, rad, pair, at, GHOST + at)
        mom[...] = dot(pair[...], fcat[s])
        own = pl.ds(pl.multiple_of(s * SLOTS, SLOTS), SLOTS)
        for m in range(9):
            summed[m, own, :] = summed[m, own, :] + weighted(mom, radial, m)
        return carry

    lax.fori_loop(0, 8, outside, 0)

    occupied = jnp.concatenate(
        [jnp.where(slot < counts[x, y : y + 1, z : z + 1], 1.0, 0.0) for x, y, z in CELLS], axis=0
    )
    mixed = []
    for l, span in enumerate((slice(0, 1), slice(1, 4), slice(4, 9))):
        part = summed[span].reshape((span.stop - span.start) * LANES, LANES)
        part = dot_split(part, mix[l])
        mixed += [part[i * LANES : (i + 1) * LANES] for i in range(span.stop - span.start)]
    q0 = mixed[0]
    q1 = sum(v * v for v in mixed[1:4])
    q2 = sum(v * v for v in mixed[4:9])
    r0, r1, r2, r3 = (readout[i : i + 1, :] for i in range(4))
    layer = q0 * r0 + q1 * r1 + q2 * r2 + (q0 * q1) * r3
    layer = jnp.sum(jnp.transpose(layer), axis=0, keepdims=True)
    lane16 = lax.broadcasted_iota(jnp.int32, (1, SLOTS), 1)
    for q, (x, y, z) in enumerate(CELLS):
        kind = species[x, y, z : z + 1, :]
        value = layer[:, q * SLOTS : (q + 1) * SLOTS]
        for k in range(table.shape[0]):
            value = value + jnp.where(kind == k, table[k], 0.0)
        energy_ref[x, y, z : z + 1, :] = jnp.where(lane16 < counts[x, y : y + 1, z : z + 1], value, 0.0)
    slope1 = 2.0 * occupied * (r1 + q0 * r3)
    slope2 = 2.0 * occupied * r2
    back = [occupied * (r0 + q1 * r3)]
    back += [v * slope1 for v in mixed[1:4]]
    back += [v * slope2 for v in mixed[4:9]]
    for l, span in enumerate((slice(0, 1), slice(1, 4), slice(4, 9))):
        part = dot_split(jnp.concatenate(back[span], axis=0), mix[l], 1)
        summed[span] = part.reshape(span.stop - span.start, LANES, LANES)

    def backward(s, carry):
        own = pl.ds(pl.multiple_of(s * SLOTS, SLOTS), SLOTS)
        for m in range(9):
            slope = summed[m, own, :]
            l = DEGREE_OF[m]
            for n in range(BASIS):
                rows = slice((n * 9 + m) * SLOTS, (n * 9 + m + 1) * SLOTS)
                high, low = halves(slope * radial[l, n : n + 1, :])
                gpair[rows, 0:128] = high
                gpair[rows, 128:256] = low
                gpair[rows, 256:384] = high
        dpair[...] = dot(gpair[...], fback[s], 1)
        pull = [None] * 3
        for chunk in range(CHUNKS):
            at = slice(chunk * LANES, (chunk + 1) * LANES)
            ux, uy, uz, inverse = (geo[s, a, :, at] for a in range(4))
            harmonic = harmonics(ux, uy, uz)
            amp = [None] * 9
            along = None
            for n in range(BASIS):
                value, slope = rad[s, n, :, at], rad[s, BASIS + n, :, at]
                inner = None
                for m in range(9):
                    part = dpair[(n * 9 + m) * SLOTS : (n * 9 + m + 1) * SLOTS, at]
                    if m > 0:
                        amp[m] = part * value if n == 0 else amp[m] + part * value
                    inner = part if m == 0 else inner + part * harmonic[m]
                along = inner * slope if n == 0 else along + inner * slope
            vx = R3 * amp[1] + R15 * (uy * amp[4] + uz * amp[7] + ux * amp[8]) - R5 * (ux * amp[6])
            vy = R3 * amp[2] + R15 * (ux * amp[4] + uz * amp[5] - uy * amp[8]) - R5 * (uy * amp[6])
            vz = R3 * amp[3] + R15 * (uy * amp[5] + ux * amp[7]) + (2.0 * R5) * (uz * amp[6])
            central = along - inverse * (ux * vx + uy * vy + uz * vz)
            for a, (u, v) in enumerate(((ux, vx), (uy, vy), (uz, vz))):
                slope = u * central + inverse * v
                ngrad[s, a : a + 1, at] = jnp.sum(slope, axis=0, keepdims=True)
                pull[a] = slope if chunk == 0 else pull[a] + slope
        for a in range(3):
            center[a, own, :] = pull[a]
        return carry

    lax.fori_loop(0, 8, backward, 0)

    for a in range(3):
        grads[SELF, a : a + 1, :] = -jnp.sum(jnp.transpose(center[a]), axis=0, keepdims=True)
    for s in range(8):
        for chunk in range(CHUNKS):
            whole = ngrad[s, :, chunk * LANES : (chunk + 1) * LANES]
            for (domain, turn), places in grouped(TABLES[s], chunk):
                piece = whole if len(places) == 8 else jnp.where(places_mask(places), whole, 0.0)
                if turn:
                    piece = pltpu.roll(piece, (8 - turn) * SLOTS, 1)
                grads[domain] = grads[domain] + piece

    copies = []
    for domain in range(27):
        if domain != SELF:
            copies.append(
                pltpu.make_async_remote_copy(
                    grads.at[domain], landed.at[26 - domain], back_sends.at[domain],
                    back_recvs.at[26 - domain], device_id=neighbour(domain), device_id_type=MESH,
                )
            )
    for copy in copies:
        copy.start()
    for copy in copies:
        copy.wait()
    total = grads[SELF]
    for domain in range(27):
        if domain != SELF:
            total = total + landed[domain]
    total = -total
    for q, (x, y, z) in enumerate(CELLS):
        force_ref[x, y, :, z, :] = total[0:3, q * SLOTS : (q + 1) * SLOTS]


VMEM = pl.BlockSpec(memory_space=pltpu.VMEM)
HBM = pl.BlockSpec(memory_space=pltpu.HBM)


def per_device(positions, features, species, counts, species_energy, radial_weight, mix_weight, readout):
    energies, forces = pl.pallas_call(
        whole_kernel,
        out_shape=(
            jax.ShapeDtypeStruct((2, 2, 2, SLOTS), F32),
            jax.ShapeDtypeStruct((2, 2, 3, 2, SLOTS), F32),
        ),
        in_specs=[HBM] * 8,
        out_specs=(VMEM, VMEM),
        scratch_shapes=[
            pltpu.VMEM((2, 2, 3, 2, SLOTS), F32),
            pltpu.VMEM((2, 2, 2, SLOTS, LANES), F32),
            pltpu.VMEM((2, 2, 2, SLOTS), jnp.int32),
            pltpu.VMEM((2, 2, 2), jnp.int32),
            pltpu.SMEM(species_energy.shape, F32),
            pltpu.VMEM((3, BASIS, LANES), F32),
            pltpu.VMEM((3, LANES, LANES), F32),
            pltpu.VMEM((4, LANES), F32),
            pltpu.SemaphoreType.DMA((8,)),
            pltpu.VMEM((27, 8, LANES), F32),
            pltpu.VMEM((27, 2, 2, 2, SLOTS, LANES), F32),
            pltpu.SemaphoreType.DMA((2, 27)),
            pltpu.SemaphoreType.DMA((2, 27)),
            pltpu.VMEM((27, 8, LANES), F32),
            pltpu.SemaphoreType.DMA((27,)),
            pltpu.SemaphoreType.DMA((27,)),
            pltpu.VMEM((8, 8, NEAR), F32),
            pltpu.VMEM((LANES, LANES), F32),
            pltpu.VMEM((2 * LANES, 256), BF16),
            pltpu.VMEM((8, 2 * GHOST, 256), BF16),
            pltpu.VMEM((8, NEAR, 384), BF16),
            pltpu.VMEM((ROWS, 2 * LANES), BF16),
            pltpu.VMEM((ROWS, 2 * GHOST), BF16),
            pltpu.VMEM((ROWS, 256), F32),
            pltpu.VMEM((9, LANES, LANES), F32),
            pltpu.VMEM((8, 2 * BASIS, SLOTS, NEAR), F32),
            pltpu.VMEM((8, 4, SLOTS, NEAR), F32),
            pltpu.VMEM((ROWS, 384), BF16),
            pltpu.VMEM((ROWS, NEAR), F32),
            pltpu.VMEM((8, 8, NEAR), F32),
            pltpu.VMEM((3, LANES, LANES), F32),
            pltpu.VMEM((27, 8, LANES), F32),
        ],
        compiler_params=pltpu.CompilerParams(
            collective_id=0, has_side_effects=True, vmem_limit_bytes=60 * 2**20
        ),
    )(
        jnp.swapaxes(positions, 2, 3), features, species, counts, species_energy,
        jnp.swapaxes(radial_weight, 0, 1), mix_weight, readout,
    )
    return energies, jnp.swapaxes(forces, 2, 3)


def solution(mesh):
    grid = P("gx", "gy", "gz")
    return jax.shard_map(
        per_device,
        mesh=mesh,
        in_specs=(grid, grid, grid, grid, P(), P(), P(), P()),
        out_specs=(grid, grid),
        check_vma=False,
    )
```

```python
import math

import jax
import jax.numpy as jnp
import numpy as np
from jax import lax
from jax.experimental import pallas as pl
from jax.experimental.pallas import tpu as pltpu
from jax.sharding import PartitionSpec as P

CUTOFF = 5.0
CELL_SIDE = 5.0
SOFTENING = 0.5
BASIS = 8
SLOTS = 16
LANES = 128
CHUNKS = 4
NEAR = CHUNKS * LANES
GHOST = NEAR - LANES
ROWS = BASIS * 9 * SLOTS
DEGREE_OF = (0, 1, 1, 1, 2, 2, 2, 2, 2)
SELF = 13
MESH = pl.DeviceIdType.MESH
AXES = ("gx", "gy", "gz")
R3, R5, R15 = math.sqrt(3.0), math.sqrt(5.0), math.sqrt(15.0)
F32, BF16 = jnp.float32, jnp.bfloat16

OFFSETS = [(a, b, c) for a in (-1, 0, 1) for b in (-1, 0, 1) for c in (-1, 0, 1)]
CELLS = [(x, y, z) for x in (0, 1) for y in (0, 1) for z in (0, 1)]


def near_table(cell):
    sign = [1 if c == 1 else -1 for c in cell]
    rim = [0 if s == 1 else 1 for s in sign]
    taken = {(0, q) for q in range(8)}
    table = [(0, q, SELF, q) for q in range(8)]
    late = []
    for size in (1, 2, 3):
        for subset in range(1, 8):
            dims = [d for d in range(3) if subset >> d & 1]
            if len(dims) != size:
                continue
            off = [sign[d] if d in dims else 0 for d in range(3)]
            domain = OFFSETS.index(tuple(off))
            for q, coords in enumerate(CELLS):
                if any(coords[d] != rim[d] for d in dims):
                    continue
                for chunk in range(1, CHUNKS):
                    if (chunk, q) not in taken:
                        taken.add((chunk, q))
                        table.append((chunk, q, domain, q))
                        break
                else:
                    late.append((domain, q))
    for domain, q in late:
        chunk, place = min(
            (c, p) for c in range(1, CHUNKS) for p in range(8) if (c, p) not in taken
        )
        taken.add((chunk, place))
        table.append((chunk, place, domain, q))
    return table


TABLES = [near_table(cell) for cell in CELLS]


def grouped(table, chunk):
    groups = {}
    for c, place, domain, q in table:
        if c == chunk:
            groups.setdefault((domain, (place - q) % 8), []).append(place)
    return sorted(groups.items())


def places_mask(places):
    lane = lax.broadcasted_iota(jnp.int32, (8, LANES), 1)
    mask = None
    for place in places:
        one = (lane >= place * SLOTS) & (lane < (place + 1) * SLOTS)
        mask = one if mask is None else mask | one
    return mask


def neighbour(domain):
    place = []
    for axis, step in zip(AXES, OFFSETS[domain]):
        count = lax.axis_size(axis)
        place.append(lax.rem(lax.axis_index(axis) + step + count, count))
    return tuple(place)


def side(domain):
    return OFFSETS[domain][0]


def rim_of(domain):
    return tuple(
        pl.ds(0, 2) if step == 0 else pl.ds(1 if step == 1 else 0, 1) for step in OFFSETS[domain]
    )


def greet():
    barrier = pltpu.get_barrier_semaphore()
    for domain in range(27):
        if domain != SELF:
            pl.semaphore_signal(
                barrier, inc=1, device_id=neighbour(domain), device_id_type=MESH
            )
    return barrier


def halves(value):
    high = value.astype(BF16)
    return high, (value - high.astype(F32)).astype(BF16)


def dot(a, b, rhs_dim=0):
    return lax.dot_general(
        a, b, (((1,), (rhs_dim,)), ((), ())), preferred_element_type=F32
    )


def dot_split(a, b, rhs_dim=0):
    a_high, a_low = halves(a)
    b_high, b_low = halves(b)
    return (
        dot(a_low, b_high, rhs_dim) + dot(a_high, b_low, rhs_dim) + dot(a_high, b_high, rhs_dim)
    )


def harmonics(ux, uy, uz):
    square = ux * ux + uy * uy + uz * uz
    return [
        None,
        R3 * ux,
        R3 * uy,
        R3 * uz,
        R15 * ux * uy,
        R15 * uy * uz,
        0.5 * R5 * (3.0 * uz * uz - square),
        R15 * ux * uz,
        0.5 * R15 * (ux * ux - uy * uy),
    ]


def radial_parts(distance, inverse, keep):
    t = jnp.minimum(distance * (1.0 / CUTOFF), 1.0)
    phi = math.pi * (t - 0.5)
    sq = phi * phi
    sine, cosine = 0.0, 0.0
    for k in range(6, -1, -1):
        if k < 6:
            sine = sine * sq + (-1) ** k / math.factorial(2 * k + 1)
        cosine = cosine * sq + (-1) ** k / math.factorial(2 * k)
    s1, c1 = cosine, -(sine * phi)
    t2 = t * t
    t4 = t2 * t2
    env = jnp.where(keep, 1.0 + t4 * t * (-21.0 + t * (35.0 - 15.0 * t)), 0.0)
    gap = 1.0 - t
    env_d = jnp.where(keep, (-105.0 / CUTOFF) * t4 * gap * gap, 0.0)
    scale = math.sqrt(2.0 / CUTOFF)
    w = scale * env * inverse
    w_d = inverse * (scale * env_d - w)
    twice = 2.0 * c1
    sines, cosines = [s1], [c1]
    for n in range(1, BASIS):
        sines.append(twice * sines[-1] - (sines[-2] if n > 1 else 0.0))
        cosines.append(twice * cosines[-1] - (cosines[-2] if n > 1 else 1.0))
    values = [s * w for s in sines]
    slopes = [
        ((n + 1) * math.pi / CUTOFF) * (c * w) + s * w_d
        for n, (s, c) in enumerate(zip(sines, cosines))
    ]
    return values, slopes


def near_pairs(s, chunk, npos, post, geo, rad, pair, high_at, low_at):
    own = pl.ds(pl.multiple_of(s * SLOTS, SLOTS), SLOTS)
    at = slice(chunk * LANES, (chunk + 1) * LANES)
    rx, ry, rz = (npos[s, a : a + 1, at] - post[own, a : a + 1] for a in range(3))
    squared = rx * rx + ry * ry + rz * rz + SOFTENING * SOFTENING
    inverse = lax.rsqrt(squared)
    distance = squared * inverse
    keep = distance < CUTOFF
    if chunk == 0:
        lane = lax.broadcasted_iota(jnp.int32, (SLOTS, LANES), 1)
        slot = lax.broadcasted_iota(jnp.int32, (SLOTS, LANES), 0)
        keep = keep & (lane != slot + s * SLOTS)
    values, slopes = radial_parts(distance, inverse, keep)
    ux, uy, uz = rx * inverse, ry * inverse, rz * inverse
    for a, part in enumerate((ux, uy, uz, inverse)):
        geo[s, a, :, at] = part
    harmonic = harmonics(ux, uy, uz)
    for n in range(BASIS):
        rad[s, n, :, at] = values[n]
        rad[s, BASIS + n, :, at] = slopes[n]
        for m in range(9):
            high, low = halves(values[n] if m == 0 else values[n] * harmonic[m])
            rows = slice((n * 9 + m) * SLOTS, (n * 9 + m + 1) * SLOTS)
            pair[rows, high_at : high_at + LANES] = high
            pair[rows, low_at : low_at + LANES] = low


def weighted(mom, radial, m):
    total = None
    for n in range(BASIS):
        rows = slice((n * 9 + m) * SLOTS, (n * 9 + m + 1) * SLOTS)
        l = DEGREE_OF[m]
        term = (mom[rows, 0:128] + mom[rows, 128:256]) * radial[l, n : n + 1, :]
        total = term if total is None else total + term
    return total


def put_near(s, chunk, npos, tiles):
    row = lax.broadcasted_iota(jnp.int32, (8, LANES), 0)
    value = jnp.full((8, LANES), 100.0, F32)
    for (domain, turn), places in grouped(TABLES[s], chunk):
        ox, oy, oz = (2.0 * CELL_SIDE * o for o in OFFSETS[domain])
        piece = tiles[domain]
        if domain != SELF:
            piece = piece + jnp.where(row == 0, ox, jnp.where(row == 1, oy, oz))
        if turn:
            piece = pltpu.roll(piece, turn * SLOTS, 1)
        value = piece if len(places) == 8 else jnp.where(places_mask(places), piece, value)
    npos[s, :, chunk * LANES : (chunk + 1) * LANES] = value


def put_forward(high, low, fcat, at, low_by):
    rows, low_rows = slice(at, at + SLOTS), slice(at + low_by, at + low_by + SLOTS)
    fcat[rows, 0:128] = high
    fcat[rows, 128:256] = low
    fcat[low_rows, 0:128] = high
    fcat[low_rows, 128:256] = jnp.zeros_like(low)


def put_backward(high, low, fback, at, low_by):
    rows, low_rows = slice(at, at + SLOTS), slice(at + low_by, at + low_by + SLOTS)
    fback[rows, 0:128] = high
    fback[rows, 128:256] = high
    fback[low_rows, 0:128] = low
    fback[low_rows, 128:256] = jnp.zeros_like(low)


def own_rows(s):
    return pl.ds(pl.multiple_of(s * SLOTS, SLOTS), SLOTS)


def over_cells(first, count, early, late):
    def step(t, carry):
        s = first + 2 * t
        early(s, 0)
        early(s + 1, 1)
        late(s, 0)
        late(s + 1, 1)
        return carry

    lax.fori_loop(0, count // 2, step, 0)


def gradient_pairs(s, summed, radial, gpair):
    for m in range(9):
        slope = summed[m, own_rows(s), :]
        l = DEGREE_OF[m]
        for n in range(BASIS):
            rows = slice((n * 9 + m) * SLOTS, (n * 9 + m + 1) * SLOTS)
            high, low = halves(slope * radial[l, n : n + 1, :])
            gpair[rows, 0:128] = high
            gpair[rows, 128:256] = low


def chunk_forces(s, chunk, dpair, high_at, low_at, geo, rad, ngrad):
    at = slice(chunk * LANES, (chunk + 1) * LANES)
    ux, uy, uz, inverse = (geo[s, a, :, at] for a in range(4))
    harmonic = harmonics(ux, uy, uz)
    amp = [None] * 9
    along = None
    for n in range(BASIS):
        value, slope = rad[s, n, :, at], rad[s, BASIS + n, :, at]
        inner = None
        for m in range(9):
            rows = slice((n * 9 + m) * SLOTS, (n * 9 + m + 1) * SLOTS)
            part = dpair[rows, high_at : high_at + LANES] + dpair[rows, low_at : low_at + LANES]
            if m > 0:
                amp[m] = part * value if n == 0 else amp[m] + part * value
            inner = part if m == 0 else inner + part * harmonic[m]
        along = inner * slope if n == 0 else along + inner * slope
    vx = R3 * amp[1] + R15 * (uy * amp[4] + uz * amp[7] + ux * amp[8]) - R5 * (ux * amp[6])
    vy = R3 * amp[2] + R15 * (ux * amp[4] + uz * amp[5] - uy * amp[8]) - R5 * (uy * amp[6])
    vz = R3 * amp[3] + R15 * (uy * amp[5] + ux * amp[7]) + (2.0 * R5) * (uz * amp[6])
    central = along - inverse * (ux * vx + uy * vy + uz * vz)
    slopes = [u * central + inverse * v for u, v in ((ux, vx), (uy, vy), (uz, vz))]
    for a in range(3):
        ngrad[s, a : a + 1, at] = jnp.sum(slopes[a], axis=0, keepdims=True)
    return slopes


def scatter(s, chunk, ngrad, grads):
    whole = ngrad[s, :, chunk * LANES : (chunk + 1) * LANES]
    for (domain, turn), places in grouped(TABLES[s], chunk):
        piece = whole if len(places) == 8 else jnp.where(places_mask(places), whole, 0.0)
        if turn:
            piece = pltpu.roll(piece, (8 - turn) * SLOTS, 1)
        grads[domain] = grads[domain] + piece


SPANS = (slice(0, 1), slice(1, 4), slice(4, 9))


def mix_half(half, slot, counts, mix, readout, summed, layers):
    rows = slice(half * 64, (half + 1) * 64)
    occupied = jnp.concatenate(
        [
            jnp.where(slot < counts[half, y : y + 1, z : z + 1], 1.0, 0.0)
            for y in (0, 1)
            for z in (0, 1)
        ],
        axis=0,
    )
    mixed = []
    for l, span in enumerate(SPANS):
        size = span.stop - span.start
        part = dot_split(summed[span, rows].reshape(size * 64, LANES), mix[l])
        mixed += [part[i * 64 : (i + 1) * 64] for i in range(size)]
    q0 = mixed[0]
    q1 = sum(v * v for v in mixed[1:4])
    q2 = sum(v * v for v in mixed[4:9])
    r0, r1, r2, r3 = (readout[i : i + 1, :] for i in range(4))
    layers[rows] = q0 * r0 + q1 * r1 + q2 * r2 + (q0 * q1) * r3
    slope1 = 2.0 * occupied * (r1 + q0 * r3)
    slope2 = 2.0 * occupied * r2
    back = [occupied * (r0 + q1 * r3)]
    back += [v * slope1 for v in mixed[1:4]]
    back += [v * slope2 for v in mixed[4:9]]
    for l, span in enumerate(SPANS):
        part = dot_split(jnp.concatenate(back[span], axis=0), mix[l], 1)
        summed[span, rows] = part.reshape(span.stop - span.start, 64, LANES)


def whole_kernel(
    pos_hbm, feat_hbm, species_hbm, counts_hbm, table_hbm, radial_hbm, mix_hbm, readout_hbm,
    energy_ref, force_ref,
    pos, feat, species, counts, table, radial, mix, readout, loads,
    tiles, feats, sends, recvs, landed, back_sends, back_recvs,
    npos, post, fown, fcat, bown, bcat, opair0, opair1, pair0, pair1, mom0, mom1,
    summed, layers, rad, geo, gpair0, gpair1, odpair0, odpair1, dpair0, dpair1,
    ngrad, center, grads,
):
    opair, pair, mom = (opair0, opair1), (pair0, pair1), (mom0, mom1)
    gpair, odpair, dpair = (gpair0, gpair1), (odpair0, odpair1), (dpair0, dpair1)
    barrier = greet()
    held = [
        pltpu.make_async_copy(source, target, loads.at[i])
        for i, (source, target) in enumerate(
            (
                (pos_hbm, pos), (counts_hbm, counts), (feat_hbm, feat), (radial_hbm, radial),
                (mix_hbm, mix), (readout_hbm, readout), (species_hbm, species), (table_hbm, table),
            )
        )
    ]
    for copy in held:
        copy.start()
    slot = lax.broadcasted_iota(jnp.int32, (SLOTS, LANES), 0)
    tiles[SELF] = jnp.zeros((8, LANES), F32)
    ngrad[...] = jnp.zeros_like(ngrad)
    grads[...] = jnp.zeros_like(grads)
    for copy in held[:3]:
        copy.wait()
    for q, (x, y, z) in enumerate(CELLS):
        tiles[SELF, 0:3, q * SLOTS : (q + 1) * SLOTS] = pos[x, y, :, z, :]
        occupied = slot < counts[x, y : y + 1, z : z + 1]
        feats[SELF, x, y, z] = jnp.where(occupied, feat[x, y, z], 0.0)
    lane = lax.broadcasted_iota(jnp.int32, (8, LANES), 1)
    row = lax.broadcasted_iota(jnp.int32, (8, LANES), 0)
    shift = jnp.where(row == 0, lane // 64, jnp.where(row == 1, lane // 32 % 2, lane // 16 % 2))
    tiles[SELF] = tiles[SELF] + CELL_SIDE * shift.astype(F32)

    halo = {}
    for domain in range(27):
        if domain == SELF:
            continue
        there, rim, back = neighbour(domain), rim_of(domain), 26 - domain
        halo[domain] = (
            pltpu.make_async_remote_copy(
                tiles.at[SELF], tiles.at[back], sends.at[0, domain], recvs.at[0, back],
                device_id=there, device_id_type=MESH,
            ),
            pltpu.make_async_remote_copy(
                feats.at[(SELF,) + rim], feats.at[(back,) + rim], sends.at[1, domain],
                recvs.at[1, back], device_id=there, device_id_type=MESH,
            ),
        )
    pl.semaphore_wait(barrier, 26)
    for step in (-1, 0, 1):
        for domain, pieces in halo.items():
            if side(domain) == step:
                for copy in pieces:
                    copy.start()

    for s in range(8):
        put_near(s, 0, npos, tiles)
    mine = tiles[SELF]
    post[...] = jnp.transpose(jnp.concatenate([mine] * 16, axis=0))
    for q, (x, y, z) in enumerate(CELLS):
        high, low = halves(feats[SELF, x, y, z])
        put_forward(high, low, fown, q * SLOTS, LANES)
        put_backward(high, low, bown, q * SLOTS, LANES)
    for copy in held[3:]:
        copy.wait()

    def own_pairs(s, b):
        near_pairs(s, 0, npos, post, geo, rad, opair[b], 0, LANES)

    def own_moments(s, b):
        mom[b][...] = dot(opair[b][...], fown[...])
        for m in range(9):
            summed[m, own_rows(s), :] = weighted(mom[b], radial, m)

    over_cells(0, 8, own_pairs, own_moments)

    def ghost_pairs(s, b):
        for chunk in range(1, CHUNKS):
            at = (chunk - 1) * LANES
            near_pairs(s, chunk, npos, post, geo, rad, pair[b], at, GHOST + at)

    def ghost_moments(s, b):
        mom[b][...] = dot(pair[b][...], fcat[s])
        for m in range(9):
            summed[m, own_rows(s), :] = summed[m, own_rows(s), :] + weighted(mom[b], radial, m)

    def ghost_gradients(s, b):
        gradient_pairs(s, summed, radial, gpair[b])
        dpair[b][...] = dot(gpair[b][...], bcat[s], 1)

    def ghost_forces(s, b):
        pull = None
        for chunk in range(1, CHUNKS):
            at = (chunk - 1) * LANES
            more = chunk_forces(s, chunk, dpair[b], at, GHOST + at, geo, rad, ngrad)
            pull = more if pull is None else [p + q for p, q in zip(pull, more)]
        for a in range(3):
            center[a, own_rows(s), :] = pull[a]

    returns = {
        domain: pltpu.make_async_remote_copy(
            grads.at[domain], landed.at[26 - domain], back_sends.at[domain],
            back_recvs.at[26 - domain], device_id=neighbour(domain), device_id_type=MESH,
        )
        for domain in range(27)
        if domain != SELF
    }
    for half in (1, 0):
        for domain, pieces in halo.items():
            if (side(domain) == 1) == (half == 0):
                for copy in pieces:
                    copy.wait_recv()
        for s in range(4 * half, 4 * half + 4):
            for chunk in range(1, CHUNKS):
                put_near(s, chunk, npos, tiles)
            filled = {(c, p): (domain, q) for c, p, domain, q in TABLES[s]}
            for chunk in range(1, CHUNKS):
                for place in range(8):
                    at = (chunk - 1) * LANES + place * SLOTS
                    if (chunk, place) in filled:
                        domain, q = filled[(chunk, place)]
                        high, low = halves(feats[(domain,) + CELLS[q]])
                    else:
                        high = low = jnp.zeros((SLOTS, LANES), BF16)
                    put_forward(high, low, fcat.at[s], at, GHOST)
                    put_backward(high, low, bcat.at[s], at, GHOST)
        over_cells(4 * half, 4, ghost_pairs, ghost_moments)
        mix_half(half, slot, counts, mix, readout, summed, layers)
        over_cells(4 * half, 4, ghost_gradients, ghost_forces)
        for s in range(4 * half, 4 * half + 4):
            for chunk in range(1, CHUNKS):
                scatter(s, chunk, ngrad, grads)
        for domain, copy in returns.items():
            if (side(domain) == 1) == (half == 1):
                copy.start()

    def own_gradients(s, b):
        gradient_pairs(s, summed, radial, gpair[b])
        odpair[b][...] = dot(gpair[b][...], bown[...], 1)

    def own_forces(s, b):
        pull = chunk_forces(s, 0, odpair[b], 0, LANES, geo, rad, ngrad)
        for a in range(3):
            center[a, own_rows(s), :] = center[a, own_rows(s), :] + pull[a]

    over_cells(0, 8, own_gradients, own_forces)
    for s in range(8):
        scatter(s, 0, ngrad, grads)
    total = grads[SELF]
    pulls = [jnp.sum(jnp.transpose(center[a]), axis=0, keepdims=True) for a in range(3)]
    total = total - jnp.concatenate(pulls + [jnp.zeros((5, LANES), F32)], axis=0)

    layer = jnp.sum(jnp.transpose(layers[...]), axis=0, keepdims=True)
    lane16 = lax.broadcasted_iota(jnp.int32, (1, SLOTS), 1)
    for q, (x, y, z) in enumerate(CELLS):
        kind = species[x, y, z : z + 1, :]
        value = layer[:, q * SLOTS : (q + 1) * SLOTS]
        for k in range(table.shape[0]):
            value = value + jnp.where(kind == k, table[k], 0.0)
        occupied = lane16 < counts[x, y : y + 1, z : z + 1]
        energy_ref[x, y, z : z + 1, :] = jnp.where(occupied, value, 0.0)

    for domain, copy in returns.items():
        copy.wait_recv()
        total = total + landed[26 - domain]
    total = -total
    for q, (x, y, z) in enumerate(CELLS):
        force_ref[x, y, :, z, :] = total[0:3, q * SLOTS : (q + 1) * SLOTS]
    for domain, pieces in halo.items():
        for copy in pieces + (returns[domain],):
            copy.wait_send()


VMEM = pl.BlockSpec(memory_space=pltpu.VMEM)
HBM = pl.BlockSpec(memory_space=pltpu.HBM)


def per_device(positions, features, species, counts, species_energy, radial_weight, mix_weight, readout):
    energies, forces = pl.pallas_call(
        whole_kernel,
        out_shape=(
            jax.ShapeDtypeStruct((2, 2, 2, SLOTS), F32),
            jax.ShapeDtypeStruct((2, 2, 3, 2, SLOTS), F32),
        ),
        in_specs=[HBM] * 8,
        out_specs=(VMEM, VMEM),
        scratch_shapes=[
            pltpu.VMEM((2, 2, 3, 2, SLOTS), F32),
            pltpu.VMEM((2, 2, 2, SLOTS, LANES), F32),
            pltpu.VMEM((2, 2, 2, SLOTS), jnp.int32),
            pltpu.VMEM((2, 2, 2), jnp.int32),
            pltpu.SMEM(species_energy.shape, F32),
            pltpu.VMEM((3, BASIS, LANES), F32),
            pltpu.VMEM((3, LANES, LANES), F32),
            pltpu.VMEM((4, LANES), F32),
            pltpu.SemaphoreType.DMA((8,)),
            pltpu.VMEM((27, 8, LANES), F32),
            pltpu.VMEM((27, 2, 2, 2, SLOTS, LANES), F32),
            pltpu.SemaphoreType.DMA((2, 27)),
            pltpu.SemaphoreType.DMA((2, 27)),
            pltpu.VMEM((27, 8, LANES), F32),
            pltpu.SemaphoreType.DMA((27,)),
            pltpu.SemaphoreType.DMA((27,)),
            pltpu.VMEM((8, 8, NEAR), F32),
            pltpu.VMEM((LANES, LANES), F32),
            pltpu.VMEM((2 * LANES, 256), BF16),
            pltpu.VMEM((8, 2 * GHOST, 256), BF16),
            pltpu.VMEM((2 * LANES, 256), BF16),
            pltpu.VMEM((8, 2 * GHOST, 256), BF16),
            pltpu.VMEM((ROWS, 2 * LANES), BF16),
            pltpu.VMEM((ROWS, 2 * LANES), BF16),
            pltpu.VMEM((ROWS, 2 * GHOST), BF16),
            pltpu.VMEM((ROWS, 2 * GHOST), BF16),
            pltpu.VMEM((ROWS, 256), F32),
            pltpu.VMEM((ROWS, 256), F32),
            pltpu.VMEM((9, LANES, LANES), F32),
            pltpu.VMEM((LANES, LANES), F32),
            pltpu.VMEM((8, 2 * BASIS, SLOTS, NEAR), F32),
            pltpu.VMEM((8, 4, SLOTS, NEAR), F32),
            pltpu.VMEM((ROWS, 256), BF16),
            pltpu.VMEM((ROWS, 256), BF16),
            pltpu.VMEM((ROWS, 2 * LANES), F32),
            pltpu.VMEM((ROWS, 2 * LANES), F32),
            pltpu.VMEM((ROWS, 2 * GHOST), F32),
            pltpu.VMEM((ROWS, 2 * GHOST), F32),
            pltpu.VMEM((8, 8, NEAR), F32),
            pltpu.VMEM((3, LANES, LANES), F32),
            pltpu.VMEM((27, 8, LANES), F32),
        ],
        compiler_params=pltpu.CompilerParams(
            collective_id=0, has_side_effects=True, vmem_limit_bytes=60 * 2**20
        ),
    )(
        jnp.swapaxes(positions, 2, 3), features, species, counts, species_energy,
        jnp.swapaxes(radial_weight, 0, 1), mix_weight, readout,
    )
    return energies, jnp.swapaxes(forces, 2, 3)


def solution(mesh):
    grid = P("gx", "gy", "gz")
    return jax.shard_map(
        per_device,
        mesh=mesh,
        in_specs=(grid, grid, grid, grid, P(), P(), P(), P()),
        out_specs=(grid, grid),
        check_vma=False,
    )
```

```python
import math

import jax
import jax.numpy as jnp
import numpy as np
from jax import lax
from jax.experimental import pallas as pl
from jax.experimental.pallas import tpu as pltpu
from jax.sharding import PartitionSpec as P

CUTOFF = 5.0
CELL_SIDE = 5.0
SOFTENING = 0.5
BASIS = 8
SLOTS = 16
LANES = 128
CHUNKS = 4
NEAR = CHUNKS * LANES
GHOST = NEAR - LANES
STEP = 4
ROWS = BASIS * 9 * SLOTS
DEGREE_OF = (0, 1, 1, 1, 2, 2, 2, 2, 2)
SELF = 13
MESH = pl.DeviceIdType.MESH
AXES = ("gx", "gy", "gz")
R3, R5, R15 = math.sqrt(3.0), math.sqrt(5.0), math.sqrt(15.0)
F32, BF16 = jnp.float32, jnp.bfloat16

OFFSETS = [(a, b, c) for a in (-1, 0, 1) for b in (-1, 0, 1) for c in (-1, 0, 1)]
CELLS = [(x, y, z) for x in (0, 1) for y in (0, 1) for z in (0, 1)]


def near_table(cell):
    sign = [1 if c == 1 else -1 for c in cell]
    rim = [0 if s == 1 else 1 for s in sign]
    taken = {(0, q) for q in range(8)}
    table = [(0, q, SELF, q) for q in range(8)]
    late = []
    for size in (1, 2, 3):
        for subset in range(1, 8):
            dims = [d for d in range(3) if subset >> d & 1]
            if len(dims) != size:
                continue
            off = [sign[d] if d in dims else 0 for d in range(3)]
            domain = OFFSETS.index(tuple(off))
            for q, coords in enumerate(CELLS):
                if any(coords[d] != rim[d] for d in dims):
                    continue
                for chunk in range(1, CHUNKS):
                    if (chunk, q) not in taken:
                        taken.add((chunk, q))
                        table.append((chunk, q, domain, q))
                        break
                else:
                    late.append((domain, q))
    for domain, q in late:
        chunk, place = min(
            (c, p) for c in range(1, CHUNKS) for p in range(8) if (c, p) not in taken
        )
        taken.add((chunk, place))
        table.append((chunk, place, domain, q))
    return table


TABLES = [near_table(cell) for cell in CELLS]


def grouped(table, chunk):
    groups = {}
    for c, place, domain, q in table:
        if c == chunk:
            groups.setdefault((domain, (place - q) % 8), []).append(place)
    return sorted(groups.items())


def places_mask(places):
    lane = lax.broadcasted_iota(jnp.int32, (8, LANES), 1)
    mask = None
    for place in places:
        one = (lane >= place * SLOTS) & (lane < (place + 1) * SLOTS)
        mask = one if mask is None else mask | one
    return mask


def neighbour(domain):
    place = []
    for axis, step in zip(AXES, OFFSETS[domain]):
        count = lax.axis_size(axis)
        place.append(lax.rem(lax.axis_index(axis) + step + count, count))
    return tuple(place)


def side(domain):
    return OFFSETS[domain][0]


def rim_of(domain):
    return tuple(
        pl.ds(0, 2) if step == 0 else pl.ds(1 if step == 1 else 0, 1) for step in OFFSETS[domain]
    )


def greet():
    barrier = pltpu.get_barrier_semaphore()
    for domain in range(27):
        if domain != SELF:
            pl.semaphore_signal(
                barrier, inc=1, device_id=neighbour(domain), device_id_type=MESH
            )
    return barrier


def halves(value):
    high = value.astype(BF16)
    return high, (value - high.astype(F32)).astype(BF16)


def dot(a, b, rhs_dim=0):
    return lax.dot_general(
        a, b, (((1,), (rhs_dim,)), ((), ())), preferred_element_type=F32
    )


def dot_split(a, b, rhs_dim=0):
    a_high, a_low = halves(a)
    b_high, b_low = halves(b)
    return (
        dot(a_low, b_high, rhs_dim) + dot(a_high, b_low, rhs_dim) + dot(a_high, b_high, rhs_dim)
    )


def harmonics(ux, uy, uz):
    square = ux * ux + uy * uy + uz * uz
    return [
        None,
        R3 * ux,
        R3 * uy,
        R3 * uz,
        R15 * ux * uy,
        R15 * uy * uz,
        0.5 * R5 * (3.0 * uz * uz - square),
        R15 * ux * uz,
        0.5 * R15 * (ux * ux - uy * uy),
    ]


def radial_parts(distance, inverse, keep):
    t = jnp.minimum(distance * (1.0 / CUTOFF), 1.0)
    phi = math.pi * (t - 0.5)
    sq = phi * phi
    sine, cosine = 0.0, 0.0
    for k in range(6, -1, -1):
        if k < 6:
            sine = sine * sq + (-1) ** k / math.factorial(2 * k + 1)
        cosine = cosine * sq + (-1) ** k / math.factorial(2 * k)
    s1, c1 = cosine, -(sine * phi)
    t2 = t * t
    t4 = t2 * t2
    env = jnp.where(keep, 1.0 + t4 * t * (-21.0 + t * (35.0 - 15.0 * t)), 0.0)
    gap = 1.0 - t
    env_d = jnp.where(keep, (-105.0 / CUTOFF) * t4 * gap * gap, 0.0)
    scale = math.sqrt(2.0 / CUTOFF)
    w = scale * env * inverse
    w_d = inverse * (scale * env_d - w)
    twice = 2.0 * c1
    sines, cosines = [s1], [c1]
    for n in range(1, BASIS):
        sines.append(twice * sines[-1] - (sines[-2] if n > 1 else 0.0))
        cosines.append(twice * cosines[-1] - (cosines[-2] if n > 1 else 1.0))
    values = [s * w for s in sines]
    slopes = [
        ((n + 1) * math.pi / CUTOFF) * (c * w) + s * w_d
        for n, (s, c) in enumerate(zip(sines, cosines))
    ]
    return values, slopes


def near_pairs(s, chunk, npos, post, geo, rad, pair, high_at, low_at):
    own = pl.ds(pl.multiple_of(s * SLOTS, SLOTS), SLOTS)
    at = slice(chunk * LANES, (chunk + 1) * LANES)
    rx, ry, rz = (npos[s, a : a + 1, at] - post[own, a : a + 1] for a in range(3))
    squared = rx * rx + ry * ry + rz * rz + SOFTENING * SOFTENING
    inverse = lax.rsqrt(squared)
    distance = squared * inverse
    keep = distance < CUTOFF
    if chunk == 0:
        lane = lax.broadcasted_iota(jnp.int32, (SLOTS, LANES), 1)
        slot = lax.broadcasted_iota(jnp.int32, (SLOTS, LANES), 0)
        keep = keep & (lane != slot + s * SLOTS)
    values, slopes = radial_parts(distance, inverse, keep)
    ux, uy, uz = rx * inverse, ry * inverse, rz * inverse
    for a, part in enumerate((ux, uy, uz, inverse)):
        geo[s, a, :, at] = part
    harmonic = harmonics(ux, uy, uz)
    for n in range(BASIS):
        rad[s, n, :, at] = values[n]
        rad[s, BASIS + n, :, at] = slopes[n]
        for m in range(9):
            high, low = halves(values[n] if m == 0 else values[n] * harmonic[m])
            rows = slice((n * 9 + m) * SLOTS, (n * 9 + m + 1) * SLOTS)
            pair[rows, high_at : high_at + LANES] = high
            pair[rows, low_at : low_at + LANES] = low


def weighted(mom, radial, m):
    total = None
    for n in range(BASIS):
        rows = slice((n * 9 + m) * SLOTS, (n * 9 + m + 1) * SLOTS)
        l = DEGREE_OF[m]
        term = (mom[rows, 0:128] + mom[rows, 128:256]) * radial[l, n : n + 1, :]
        total = term if total is None else total + term
    return total


def put_near(s, chunk, npos, tiles):
    row = lax.broadcasted_iota(jnp.int32, (8, LANES), 0)
    value = jnp.full((8, LANES), 100.0, F32)
    for (domain, turn), places in grouped(TABLES[s], chunk):
        ox, oy, oz = (2.0 * CELL_SIDE * o for o in OFFSETS[domain])
        piece = tiles[domain]
        if domain != SELF:
            piece = piece + jnp.where(row == 0, ox, jnp.where(row == 1, oy, oz))
        if turn:
            piece = pltpu.roll(piece, turn * SLOTS, 1)
        value = piece if len(places) == 8 else jnp.where(places_mask(places), piece, value)
    npos[s, :, chunk * LANES : (chunk + 1) * LANES] = value


def put_forward(high, low, fcat, at, low_by):
    rows, low_rows = slice(at, at + SLOTS), slice(at + low_by, at + low_by + SLOTS)
    fcat[rows, 0:128] = high
    fcat[rows, 128:256] = low
    fcat[low_rows, 0:128] = high
    fcat[low_rows, 128:256] = jnp.zeros_like(low)


def put_backward(high, low, fback, at, low_by):
    rows, low_rows = slice(at, at + SLOTS), slice(at + low_by, at + low_by + SLOTS)
    fback[rows, 0:128] = high
    fback[rows, 128:256] = high
    fback[low_rows, 0:128] = low
    fback[low_rows, 128:256] = jnp.zeros_like(low)


def own_rows(s):
    return pl.ds(pl.multiple_of(s * SLOTS, SLOTS), SLOTS)


def over_cells(first, count, early, late):
    def step(t, carry):
        s = first + STEP * t
        for b in range(STEP):
            early(s + b, b)
        for b in range(STEP):
            late(s + b, b)
        return carry

    lax.fori_loop(0, count // STEP, step, 0)


def gradient_pairs(s, summed, radial, gpair):
    for m in range(9):
        slope = summed[m, own_rows(s), :]
        l = DEGREE_OF[m]
        for n in range(BASIS):
            rows = slice((n * 9 + m) * SLOTS, (n * 9 + m + 1) * SLOTS)
            high, low = halves(slope * radial[l, n : n + 1, :])
            gpair[rows, 0:128] = high
            gpair[rows, 128:256] = low


def chunk_forces(s, chunk, dpair, high_at, low_at, geo, rad, ngrad):
    at = slice(chunk * LANES, (chunk + 1) * LANES)
    ux, uy, uz, inverse = (geo[s, a, :, at] for a in range(4))
    harmonic = harmonics(ux, uy, uz)
    amp = [None] * 9
    along = None
    for n in range(BASIS):
        value, slope = rad[s, n, :, at], rad[s, BASIS + n, :, at]
        inner = None
        for m in range(9):
            rows = slice((n * 9 + m) * SLOTS, (n * 9 + m + 1) * SLOTS)
            part = dpair[rows, high_at : high_at + LANES] + dpair[rows, low_at : low_at + LANES]
            if m > 0:
                amp[m] = part * value if n == 0 else amp[m] + part * value
            inner = part if m == 0 else inner + part * harmonic[m]
        along = inner * slope if n == 0 else along + inner * slope
    vx = R3 * amp[1] + R15 * (uy * amp[4] + uz * amp[7] + ux * amp[8]) - R5 * (ux * amp[6])
    vy = R3 * amp[2] + R15 * (ux * amp[4] + uz * amp[5] - uy * amp[8]) - R5 * (uy * amp[6])
    vz = R3 * amp[3] + R15 * (uy * amp[5] + ux * amp[7]) + (2.0 * R5) * (uz * amp[6])
    central = along - inverse * (ux * vx + uy * vy + uz * vz)
    slopes = [u * central + inverse * v for u, v in ((ux, vx), (uy, vy), (uz, vz))]
    for a in range(3):
        ngrad[s, a : a + 1, at] = jnp.sum(slopes[a], axis=0, keepdims=True)
    return slopes


def scatter(s, chunk, ngrad, grads):
    whole = ngrad[s, :, chunk * LANES : (chunk + 1) * LANES]
    for (domain, turn), places in grouped(TABLES[s], chunk):
        piece = whole if len(places) == 8 else jnp.where(places_mask(places), whole, 0.0)
        if turn:
            piece = pltpu.roll(piece, (8 - turn) * SLOTS, 1)
        grads[domain] = grads[domain] + piece


SPANS = (slice(0, 1), slice(1, 4), slice(4, 9))


def mix_half(half, slot, counts, mix, readout, summed, layers):
    rows = slice(half * 64, (half + 1) * 64)
    occupied = jnp.concatenate(
        [
            jnp.where(slot < counts[half, y : y + 1, z : z + 1], 1.0, 0.0)
            for y in (0, 1)
            for z in (0, 1)
        ],
        axis=0,
    )
    mixed = []
    for l, span in enumerate(SPANS):
        size = span.stop - span.start
        part = dot_split(summed[span, rows].reshape(size * 64, LANES), mix[l])
        mixed += [part[i * 64 : (i + 1) * 64] for i in range(size)]
    q0 = mixed[0]
    q1 = sum(v * v for v in mixed[1:4])
    q2 = sum(v * v for v in mixed[4:9])
    r0, r1, r2, r3 = (readout[i : i + 1, :] for i in range(4))
    layers[rows] = q0 * r0 + q1 * r1 + q2 * r2 + (q0 * q1) * r3
    slope1 = 2.0 * occupied * (r1 + q0 * r3)
    slope2 = 2.0 * occupied * r2
    back = [occupied * (r0 + q1 * r3)]
    back += [v * slope1 for v in mixed[1:4]]
    back += [v * slope2 for v in mixed[4:9]]
    for l, span in enumerate(SPANS):
        part = dot_split(jnp.concatenate(back[span], axis=0), mix[l], 1)
        summed[span, rows] = part.reshape(span.stop - span.start, 64, LANES)


def whole_kernel(
    pos_hbm, feat_hbm, species_hbm, counts_hbm, table_hbm, radial_hbm, mix_hbm, readout_hbm,
    energy_ref, force_ref,
    pos, feat, species, counts, table, radial, mix, readout, loads,
    tiles, feats, sends, recvs, landed, back_sends, back_recvs,
    npos, post, fown, fcat, bown, bcat, summed, layers, rad, geo, ngrad, center, grads,
    *buffers,
):
    opair, pair, mom, gpair, odpair, dpair = (
        buffers[i * STEP : (i + 1) * STEP] for i in range(6)
    )
    barrier = greet()
    held = [
        pltpu.make_async_copy(source, target, loads.at[i])
        for i, (source, target) in enumerate(
            (
                (pos_hbm, pos), (counts_hbm, counts), (feat_hbm, feat), (radial_hbm, radial),
                (mix_hbm, mix), (readout_hbm, readout), (species_hbm, species), (table_hbm, table),
            )
        )
    ]
    for copy in held:
        copy.start()
    slot = lax.broadcasted_iota(jnp.int32, (SLOTS, LANES), 0)
    tiles[SELF] = jnp.zeros((8, LANES), F32)
    ngrad[...] = jnp.zeros_like(ngrad)
    grads[...] = jnp.zeros_like(grads)
    for copy in held[:3]:
        copy.wait()
    for q, (x, y, z) in enumerate(CELLS):
        tiles[SELF, 0:3, q * SLOTS : (q + 1) * SLOTS] = pos[x, y, :, z, :]
        occupied = slot < counts[x, y : y + 1, z : z + 1]
        feats[SELF, x, y, z] = jnp.where(occupied, feat[x, y, z], 0.0)
    lane = lax.broadcasted_iota(jnp.int32, (8, LANES), 1)
    row = lax.broadcasted_iota(jnp.int32, (8, LANES), 0)
    shift = jnp.where(row == 0, lane // 64, jnp.where(row == 1, lane // 32 % 2, lane // 16 % 2))
    tiles[SELF] = tiles[SELF] + CELL_SIDE * shift.astype(F32)

    halo = {}
    for domain in range(27):
        if domain == SELF:
            continue
        there, rim, back = neighbour(domain), rim_of(domain), 26 - domain
        halo[domain] = (
            pltpu.make_async_remote_copy(
                tiles.at[SELF], tiles.at[back], sends.at[0, domain], recvs.at[0, back],
                device_id=there, device_id_type=MESH,
            ),
            pltpu.make_async_remote_copy(
                feats.at[(SELF,) + rim], feats.at[(back,) + rim], sends.at[1, domain],
                recvs.at[1, back], device_id=there, device_id_type=MESH,
            ),
        )

    def send_halo():
        pl.semaphore_wait(barrier, 26)
        for step in (-1, 0, 1):
            for domain, pieces in halo.items():
                if side(domain) == step:
                    for copy in pieces:
                        copy.start()

    planes = max(lax.axis_size("gx") // 2, 1)
    early = lax.rem(lax.axis_index("gx"), planes) == 0
    pl.when(jnp.logical_not(early))(send_halo)

    for s in range(8):
        put_near(s, 0, npos, tiles)
    mine = tiles[SELF]
    post[...] = jnp.transpose(jnp.concatenate([mine] * 16, axis=0))
    for q, (x, y, z) in enumerate(CELLS):
        high, low = halves(feats[SELF, x, y, z])
        put_forward(high, low, fown, q * SLOTS, LANES)
        put_backward(high, low, bown, q * SLOTS, LANES)
    for copy in held[3:]:
        copy.wait()

    def own_pairs(s, b):
        near_pairs(s, 0, npos, post, geo, rad, opair[b], 0, LANES)

    def own_moments(s, b):
        mom[b][...] = dot(opair[b][...], fown[...])
        for m in range(9):
            summed[m, own_rows(s), :] = weighted(mom[b], radial, m)

    over_cells(0, 8, own_pairs, own_moments)
    pl.when(early)(send_halo)

    def ghost_pairs(s, b):
        for chunk in range(1, CHUNKS):
            at = (chunk - 1) * LANES
            near_pairs(s, chunk, npos, post, geo, rad, pair[b], at, GHOST + at)

    def ghost_moments(s, b):
        mom[b][...] = dot(pair[b][...], fcat[s])
        for m in range(9):
            summed[m, own_rows(s), :] = summed[m, own_rows(s), :] + weighted(mom[b], radial, m)

    def ghost_gradients(s, b):
        gradient_pairs(s, summed, radial, gpair[b])
        dpair[b][...] = dot(gpair[b][...], bcat[s], 1)

    def ghost_forces(s, b):
        pull = None
        for chunk in range(1, CHUNKS):
            at = (chunk - 1) * LANES
            more = chunk_forces(s, chunk, dpair[b], at, GHOST + at, geo, rad, ngrad)
            pull = more if pull is None else [p + q for p, q in zip(pull, more)]
        for a in range(3):
            center[a, own_rows(s), :] = pull[a]

    returns = {
        domain: pltpu.make_async_remote_copy(
            grads.at[domain], landed.at[26 - domain], back_sends.at[domain],
            back_recvs.at[26 - domain], device_id=neighbour(domain), device_id_type=MESH,
        )
        for domain in range(27)
        if domain != SELF
    }
    for half in (1, 0):
        for domain, pieces in halo.items():
            if (side(domain) == 1) == (half == 0):
                for copy in pieces:
                    copy.wait_recv()
        for s in range(4 * half, 4 * half + 4):
            for chunk in range(1, CHUNKS):
                put_near(s, chunk, npos, tiles)
            filled = {(c, p): (domain, q) for c, p, domain, q in TABLES[s]}
            for chunk in range(1, CHUNKS):
                for place in range(8):
                    at = (chunk - 1) * LANES + place * SLOTS
                    if (chunk, place) in filled:
                        domain, q = filled[(chunk, place)]
                        high, low = halves(feats[(domain,) + CELLS[q]])
                    else:
                        high = low = jnp.zeros((SLOTS, LANES), BF16)
                    put_forward(high, low, fcat.at[s], at, GHOST)
                    put_backward(high, low, bcat.at[s], at, GHOST)
        over_cells(4 * half, 4, ghost_pairs, ghost_moments)
        mix_half(half, slot, counts, mix, readout, summed, layers)
        over_cells(4 * half, 4, ghost_gradients, ghost_forces)
        for s in range(4 * half, 4 * half + 4):
            for chunk in range(1, CHUNKS):
                scatter(s, chunk, ngrad, grads)
        for domain, copy in returns.items():
            if (side(domain) == 1) == (half == 1):
                copy.start()

    def own_gradients(s, b):
        gradient_pairs(s, summed, radial, gpair[b])
        odpair[b][...] = dot(gpair[b][...], bown[...], 1)

    def own_forces(s, b):
        pull = chunk_forces(s, 0, odpair[b], 0, LANES, geo, rad, ngrad)
        for a in range(3):
            center[a, own_rows(s), :] = center[a, own_rows(s), :] + pull[a]

    over_cells(0, 8, own_gradients, own_forces)
    for s in range(8):
        scatter(s, 0, ngrad, grads)
    total = grads[SELF]
    pulls = [jnp.sum(jnp.transpose(center[a]), axis=0, keepdims=True) for a in range(3)]
    total = total - jnp.concatenate(pulls + [jnp.zeros((5, LANES), F32)], axis=0)

    layer = jnp.sum(jnp.transpose(layers[...]), axis=0, keepdims=True)
    lane16 = lax.broadcasted_iota(jnp.int32, (1, SLOTS), 1)
    for q, (x, y, z) in enumerate(CELLS):
        kind = species[x, y, z : z + 1, :]
        value = layer[:, q * SLOTS : (q + 1) * SLOTS]
        for k in range(table.shape[0]):
            value = value + jnp.where(kind == k, table[k], 0.0)
        occupied = lane16 < counts[x, y : y + 1, z : z + 1]
        energy_ref[x, y, z : z + 1, :] = jnp.where(occupied, value, 0.0)

    for domain, copy in returns.items():
        copy.wait_recv()
        total = total + landed[26 - domain]
    total = -total
    for q, (x, y, z) in enumerate(CELLS):
        force_ref[x, y, :, z, :] = total[0:3, q * SLOTS : (q + 1) * SLOTS]
    for domain, pieces in halo.items():
        for copy in pieces + (returns[domain],):
            copy.wait_send()


VMEM = pl.BlockSpec(memory_space=pltpu.VMEM)
HBM = pl.BlockSpec(memory_space=pltpu.HBM)


def per_device(positions, features, species, counts, species_energy, radial_weight, mix_weight, readout):
    energies, forces = pl.pallas_call(
        whole_kernel,
        out_shape=(
            jax.ShapeDtypeStruct((2, 2, 2, SLOTS), F32),
            jax.ShapeDtypeStruct((2, 2, 3, 2, SLOTS), F32),
        ),
        in_specs=[HBM] * 8,
        out_specs=(VMEM, VMEM),
        scratch_shapes=[
            pltpu.VMEM((2, 2, 3, 2, SLOTS), F32),
            pltpu.VMEM((2, 2, 2, SLOTS, LANES), F32),
            pltpu.VMEM((2, 2, 2, SLOTS), jnp.int32),
            pltpu.VMEM((2, 2, 2), jnp.int32),
            pltpu.SMEM(species_energy.shape, F32),
            pltpu.VMEM((3, BASIS, LANES), F32),
            pltpu.VMEM((3, LANES, LANES), F32),
            pltpu.VMEM((4, LANES), F32),
            pltpu.SemaphoreType.DMA((8,)),
            pltpu.VMEM((27, 8, LANES), F32),
            pltpu.VMEM((27, 2, 2, 2, SLOTS, LANES), F32),
            pltpu.SemaphoreType.DMA((2, 27)),
            pltpu.SemaphoreType.DMA((2, 27)),
            pltpu.VMEM((27, 8, LANES), F32),
            pltpu.SemaphoreType.DMA((27,)),
            pltpu.SemaphoreType.DMA((27,)),
            pltpu.VMEM((8, 8, NEAR), F32),
            pltpu.VMEM((LANES, LANES), F32),
            pltpu.VMEM((2 * LANES, 256), BF16),
            pltpu.VMEM((8, 2 * GHOST, 256), BF16),
            pltpu.VMEM((2 * LANES, 256), BF16),
            pltpu.VMEM((8, 2 * GHOST, 256), BF16),
            pltpu.VMEM((9, LANES, LANES), F32),
            pltpu.VMEM((LANES, LANES), F32),
            pltpu.VMEM((8, 2 * BASIS, SLOTS, NEAR), F32),
            pltpu.VMEM((8, 4, SLOTS, NEAR), F32),
            pltpu.VMEM((8, 8, NEAR), F32),
            pltpu.VMEM((3, LANES, LANES), F32),
            pltpu.VMEM((27, 8, LANES), F32),
            *[pltpu.VMEM((ROWS, 2 * LANES), BF16)] * STEP,
            *[pltpu.VMEM((ROWS, 2 * GHOST), BF16)] * STEP,
            *[pltpu.VMEM((ROWS, 256), F32)] * STEP,
            *[pltpu.VMEM((ROWS, 256), BF16)] * STEP,
            *[pltpu.VMEM((ROWS, 2 * LANES), F32)] * STEP,
            *[pltpu.VMEM((ROWS, 2 * GHOST), F32)] * STEP,
        ],
        compiler_params=pltpu.CompilerParams(
            collective_id=0, has_side_effects=True, vmem_limit_bytes=60 * 2**20
        ),
    )(
        jnp.swapaxes(positions, 2, 3), features, species, counts, species_energy,
        jnp.swapaxes(radial_weight, 0, 1), mix_weight, readout,
    )
    return energies, jnp.swapaxes(forces, 2, 3)


def solution(mesh):
    grid = P("gx", "gy", "gz")
    return jax.shard_map(
        per_device,
        mesh=mesh,
        in_specs=(grid, grid, grid, grid, P(), P(), P(), P()),
        out_specs=(grid, grid),
        check_vma=False,
    )
```

```python
import math

import jax
import jax.numpy as jnp
import numpy as np
from jax import lax
from jax.experimental import pallas as pl
from jax.experimental.pallas import tpu as pltpu
from jax.sharding import PartitionSpec as P

CUTOFF = 5.0
CELL_SIDE = 5.0
SOFTENING = 0.5
BASIS = 8
SLOTS = 16
LANES = 128
CHUNKS = 4
NEAR = CHUNKS * LANES
GHOST = NEAR - LANES
STEP = 4
TILE = 4
ROWS = BASIS * 9 * SLOTS
DEGREE_OF = (0, 1, 1, 1, 2, 2, 2, 2, 2)
SELF = 13
MESH = pl.DeviceIdType.MESH
AXES = ("gx", "gy", "gz")
R3, R5, R15 = math.sqrt(3.0), math.sqrt(5.0), math.sqrt(15.0)
F32, BF16 = jnp.float32, jnp.bfloat16

OFFSETS = [(a, b, c) for a in (-1, 0, 1) for b in (-1, 0, 1) for c in (-1, 0, 1)]
CELLS = [(x, y, z) for x in (0, 1) for y in (0, 1) for z in (0, 1)]


def near_table(cell):
    sign = [1 if c == 1 else -1 for c in cell]
    rim = [0 if s == 1 else 1 for s in sign]
    taken = {(0, q) for q in range(8)}
    table = [(0, q, SELF, q) for q in range(8)]
    late = []
    for size in (1, 2, 3):
        for subset in range(1, 8):
            dims = [d for d in range(3) if subset >> d & 1]
            if len(dims) != size:
                continue
            off = [sign[d] if d in dims else 0 for d in range(3)]
            domain = OFFSETS.index(tuple(off))
            for q, coords in enumerate(CELLS):
                if any(coords[d] != rim[d] for d in dims):
                    continue
                for chunk in range(1, CHUNKS):
                    if (chunk, q) not in taken:
                        taken.add((chunk, q))
                        table.append((chunk, q, domain, q))
                        break
                else:
                    late.append((domain, q))
    for domain, q in late:
        chunk, place = min(
            (c, p) for c in range(1, CHUNKS) for p in range(8) if (c, p) not in taken
        )
        taken.add((chunk, place))
        table.append((chunk, place, domain, q))
    return table


TABLES = [near_table(cell) for cell in CELLS]


def grouped(table, chunk):
    groups = {}
    for c, place, domain, q in table:
        if c == chunk:
            groups.setdefault((domain, (place - q) % 8), []).append(place)
    return sorted(groups.items())


def places_mask(places):
    lane = lax.broadcasted_iota(jnp.int32, (TILE, LANES), 1)
    mask = None
    for place in places:
        one = (lane >= place * SLOTS) & (lane < (place + 1) * SLOTS)
        mask = one if mask is None else mask | one
    return mask


def neighbour(domain):
    place = []
    for axis, step in zip(AXES, OFFSETS[domain]):
        count = lax.axis_size(axis)
        place.append(lax.rem(lax.axis_index(axis) + step + count, count))
    return tuple(place)


def side(domain):
    return OFFSETS[domain][0]


def rim_of(domain):
    return tuple(
        pl.ds(0, 2) if step == 0 else pl.ds(1 if step == 1 else 0, 1) for step in OFFSETS[domain]
    )


def greet():
    barrier = pltpu.get_barrier_semaphore()
    for domain in range(27):
        if domain != SELF:
            pl.semaphore_signal(
                barrier, inc=1, device_id=neighbour(domain), device_id_type=MESH
            )
    return barrier


def halves(value):
    high = value.astype(BF16)
    return high, (value - high.astype(F32)).astype(BF16)


def dot(a, b, rhs_dim=0):
    return lax.dot_general(
        a, b, (((1,), (rhs_dim,)), ((), ())), preferred_element_type=F32
    )


def dot_split(a, b, rhs_dim=0):
    a_high, a_low = halves(a)
    b_high, b_low = halves(b)
    return (
        dot(a_low, b_high, rhs_dim) + dot(a_high, b_low, rhs_dim) + dot(a_high, b_high, rhs_dim)
    )


def harmonics(ux, uy, uz):
    square = ux * ux + uy * uy + uz * uz
    return [
        None,
        R3 * ux,
        R3 * uy,
        R3 * uz,
        R15 * ux * uy,
        R15 * uy * uz,
        0.5 * R5 * (3.0 * uz * uz - square),
        R15 * ux * uz,
        0.5 * R15 * (ux * ux - uy * uy),
    ]


def radial_parts(distance, inverse, keep):
    t = jnp.minimum(distance * (1.0 / CUTOFF), 1.0)
    phi = math.pi * (t - 0.5)
    sq = phi * phi
    sine, cosine = 0.0, 0.0
    for k in range(6, -1, -1):
        if k < 6:
            sine = sine * sq + (-1) ** k / math.factorial(2 * k + 1)
        cosine = cosine * sq + (-1) ** k / math.factorial(2 * k)
    s1, c1 = cosine, -(sine * phi)
    t2 = t * t
    t4 = t2 * t2
    env = jnp.where(keep, 1.0 + t4 * t * (-21.0 + t * (35.0 - 15.0 * t)), 0.0)
    gap = 1.0 - t
    env_d = jnp.where(keep, (-105.0 / CUTOFF) * t4 * gap * gap, 0.0)
    scale = math.sqrt(2.0 / CUTOFF)
    w = scale * env * inverse
    w_d = inverse * (scale * env_d - w)
    twice = 2.0 * c1
    sines, cosines = [s1], [c1]
    for n in range(1, BASIS):
        sines.append(twice * sines[-1] - (sines[-2] if n > 1 else 0.0))
        cosines.append(twice * cosines[-1] - (cosines[-2] if n > 1 else 1.0))
    values = [s * w for s in sines]
    slopes = [
        ((n + 1) * math.pi / CUTOFF) * (c * w) + s * w_d
        for n, (s, c) in enumerate(zip(sines, cosines))
    ]
    return values, slopes


def near_pairs(s, chunk, npos, post, geo, rad, pair, high_at, low_at):
    own = pl.ds(pl.multiple_of(s * SLOTS, SLOTS), SLOTS)
    at = slice(chunk * LANES, (chunk + 1) * LANES)
    rx, ry, rz = (npos[s, a : a + 1, at] - post[own, a : a + 1] for a in range(3))
    squared = rx * rx + ry * ry + rz * rz + SOFTENING * SOFTENING
    inverse = lax.rsqrt(squared)
    distance = squared * inverse
    keep = distance < CUTOFF
    if chunk == 0:
        lane = lax.broadcasted_iota(jnp.int32, (SLOTS, LANES), 1)
        slot = lax.broadcasted_iota(jnp.int32, (SLOTS, LANES), 0)
        keep = keep & (lane != slot + s * SLOTS)
    values, slopes = radial_parts(distance, inverse, keep)
    ux, uy, uz = rx * inverse, ry * inverse, rz * inverse
    for a, part in enumerate((ux, uy, uz, inverse)):
        geo[s, a, :, at] = part
    harmonic = harmonics(ux, uy, uz)
    for n in range(BASIS):
        rad[s, n, :, at] = values[n]
        rad[s, BASIS + n, :, at] = slopes[n]
        for m in range(9):
            high, low = halves(values[n] if m == 0 else values[n] * harmonic[m])
            rows = slice((n * 9 + m) * SLOTS, (n * 9 + m + 1) * SLOTS)
            pair[rows, high_at : high_at + LANES] = high
            pair[rows, low_at : low_at + LANES] = low


def weighted(mom, radial, m):
    total = None
    for n in range(BASIS):
        rows = slice((n * 9 + m) * SLOTS, (n * 9 + m + 1) * SLOTS)
        l = DEGREE_OF[m]
        term = (mom[rows, 0:128] + mom[rows, 128:256]) * radial[l, n : n + 1, :]
        total = term if total is None else total + term
    return total


def put_near(s, chunk, npos, tiles):
    row = lax.broadcasted_iota(jnp.int32, (TILE, LANES), 0)
    value = jnp.full((TILE, LANES), 100.0, F32)
    for (domain, turn), places in grouped(TABLES[s], chunk):
        ox, oy, oz = (2.0 * CELL_SIDE * o for o in OFFSETS[domain])
        piece = tiles[domain]
        if domain != SELF:
            piece = piece + jnp.where(row == 0, ox, jnp.where(row == 1, oy, oz))
        if turn:
            piece = pltpu.roll(piece, turn * SLOTS, 1)
        value = piece if len(places) == 8 else jnp.where(places_mask(places), piece, value)
    npos[s, :, chunk * LANES : (chunk + 1) * LANES] = value


def put_forward(high, low, fcat, at, low_by):
    rows, low_rows = slice(at, at + SLOTS), slice(at + low_by, at + low_by + SLOTS)
    fcat[rows, 0:128] = high
    fcat[rows, 128:256] = low
    fcat[low_rows, 0:128] = high
    fcat[low_rows, 128:256] = jnp.zeros_like(low)


def put_backward(high, low, fback, at, low_by):
    rows, low_rows = slice(at, at + SLOTS), slice(at + low_by, at + low_by + SLOTS)
    fback[rows, 0:128] = high
    fback[rows, 128:256] = high
    fback[low_rows, 0:128] = low
    fback[low_rows, 128:256] = jnp.zeros_like(low)


def own_rows(s):
    return pl.ds(pl.multiple_of(s * SLOTS, SLOTS), SLOTS)


def over_cells(first, count, *works):
    def step(t, carry):
        s = first + STEP * t
        for work in works:
            for b in range(STEP):
                work(s + b, b)
        return carry

    lax.fori_loop(0, count // STEP, step, 0)


def gradient_pairs(s, summed, radial, gpair):
    for m in range(9):
        slope = summed[m, own_rows(s), :]
        l = DEGREE_OF[m]
        for n in range(BASIS):
            rows = slice((n * 9 + m) * SLOTS, (n * 9 + m + 1) * SLOTS)
            high, low = halves(slope * radial[l, n : n + 1, :])
            gpair[rows, 0:128] = high
            gpair[rows, 128:256] = low


def chunk_forces(s, chunk, dpair, high_at, low_at, geo, rad, ngrad):
    at = slice(chunk * LANES, (chunk + 1) * LANES)
    ux, uy, uz, inverse = (geo[s, a, :, at] for a in range(4))
    harmonic = harmonics(ux, uy, uz)
    amp = [None] * 9
    along = None
    for n in range(BASIS):
        value, slope = rad[s, n, :, at], rad[s, BASIS + n, :, at]
        inner = None
        for m in range(9):
            rows = slice((n * 9 + m) * SLOTS, (n * 9 + m + 1) * SLOTS)
            part = dpair[rows, high_at : high_at + LANES] + dpair[rows, low_at : low_at + LANES]
            if m > 0:
                amp[m] = part * value if n == 0 else amp[m] + part * value
            inner = part if m == 0 else inner + part * harmonic[m]
        along = inner * slope if n == 0 else along + inner * slope
    vx = R3 * amp[1] + R15 * (uy * amp[4] + uz * amp[7] + ux * amp[8]) - R5 * (ux * amp[6])
    vy = R3 * amp[2] + R15 * (ux * amp[4] + uz * amp[5] - uy * amp[8]) - R5 * (uy * amp[6])
    vz = R3 * amp[3] + R15 * (uy * amp[5] + ux * amp[7]) + (2.0 * R5) * (uz * amp[6])
    central = along - inverse * (ux * vx + uy * vy + uz * vz)
    slopes = [u * central + inverse * v for u, v in ((ux, vx), (uy, vy), (uz, vz))]
    for a in range(3):
        ngrad[s, a : a + 1, at] = jnp.sum(slopes[a], axis=0, keepdims=True)
    return slopes


def scatter(s, chunk, ngrad, grads):
    whole = ngrad[s, :, chunk * LANES : (chunk + 1) * LANES]
    for (domain, turn), places in grouped(TABLES[s], chunk):
        piece = whole if len(places) == 8 else jnp.where(places_mask(places), whole, 0.0)
        if turn:
            piece = pltpu.roll(piece, (8 - turn) * SLOTS, 1)
        grads[domain] = grads[domain] + piece


SPANS = (slice(0, 1), slice(1, 4), slice(4, 9))


def mix_half(half, slot, counts, mix, readout, summed, layers):
    rows = slice(half * 64, (half + 1) * 64)
    occupied = jnp.concatenate(
        [
            jnp.where(slot < counts[half, y : y + 1, z : z + 1], 1.0, 0.0)
            for y in (0, 1)
            for z in (0, 1)
        ],
        axis=0,
    )
    mixed = []
    for l, span in enumerate(SPANS):
        size = span.stop - span.start
        part = dot_split(summed[span, rows].reshape(size * 64, LANES), mix[l])
        mixed += [part[i * 64 : (i + 1) * 64] for i in range(size)]
    q0 = mixed[0]
    q1 = sum(v * v for v in mixed[1:4])
    q2 = sum(v * v for v in mixed[4:9])
    r0, r1, r2, r3 = (readout[i : i + 1, :] for i in range(4))
    layers[rows] = q0 * r0 + q1 * r1 + q2 * r2 + (q0 * q1) * r3
    slope1 = 2.0 * occupied * (r1 + q0 * r3)
    slope2 = 2.0 * occupied * r2
    back = [occupied * (r0 + q1 * r3)]
    back += [v * slope1 for v in mixed[1:4]]
    back += [v * slope2 for v in mixed[4:9]]
    for l, span in enumerate(SPANS):
        part = dot_split(jnp.concatenate(back[span], axis=0), mix[l], 1)
        summed[span, rows] = part.reshape(span.stop - span.start, 64, LANES)


def whole_kernel(
    pos_hbm, feat_hbm, species_hbm, counts_hbm, table_hbm, radial_hbm, mix_hbm, readout_hbm,
    energy_ref, force_ref,
    pos, feat, species, counts, table, radial, mix, readout, loads,
    tiles, feats, sends, recvs, landed, back_sends, back_recvs,
    npos, post, fown, fcat, bown, bcat, summed, layers, rad, geo, ngrad, center, grads,
    *buffers,
):
    opair, pair, mom, gpair, odpair, dpair = (
        buffers[i * STEP : (i + 1) * STEP] for i in range(6)
    )
    barrier = greet()
    held = [
        pltpu.make_async_copy(source, target, loads.at[i])
        for i, (source, target) in enumerate(
            (
                (pos_hbm, pos), (counts_hbm, counts), (feat_hbm, feat), (radial_hbm, radial),
                (mix_hbm, mix), (readout_hbm, readout), (species_hbm, species), (table_hbm, table),
            )
        )
    ]
    for copy in held:
        copy.start()
    slot = lax.broadcasted_iota(jnp.int32, (SLOTS, LANES), 0)
    tiles[SELF] = jnp.zeros((TILE, LANES), F32)
    ngrad[...] = jnp.zeros_like(ngrad)
    grads[...] = jnp.zeros_like(grads)
    for copy in held[:3]:
        copy.wait()
    for q, (x, y, z) in enumerate(CELLS):
        tiles[SELF, 0:3, q * SLOTS : (q + 1) * SLOTS] = pos[x, y, :, z, :]
        occupied = slot < counts[x, y : y + 1, z : z + 1]
        feats[SELF, x, y, z] = jnp.where(occupied, feat[x, y, z], 0.0)
    lane = lax.broadcasted_iota(jnp.int32, (TILE, LANES), 1)
    row = lax.broadcasted_iota(jnp.int32, (TILE, LANES), 0)
    shift = jnp.where(row == 0, lane // 64, jnp.where(row == 1, lane // 32 % 2, lane // 16 % 2))
    tiles[SELF] = tiles[SELF] + CELL_SIDE * shift.astype(F32)

    halo = {}
    for domain in range(27):
        if domain == SELF:
            continue
        there, rim, back = neighbour(domain), rim_of(domain), 26 - domain
        halo[domain] = (
            pltpu.make_async_remote_copy(
                tiles.at[SELF], tiles.at[back], sends.at[0, domain], recvs.at[0, back],
                device_id=there, device_id_type=MESH,
            ),
            pltpu.make_async_remote_copy(
                feats.at[(SELF,) + rim], feats.at[(back,) + rim], sends.at[1, domain],
                recvs.at[1, back], device_id=there, device_id_type=MESH,
            ),
        )

    def send_halo():
        pl.semaphore_wait(barrier, 26)
        for piece in (0, 1):
            for step in (-1, 0, 1):
                for domain, pieces in halo.items():
                    if side(domain) == step:
                        pieces[piece].start()

    planes = max(lax.axis_size("gx") // 2, 1)
    early = lax.rem(lax.axis_index("gx"), planes) == 0
    pl.when(jnp.logical_not(early))(send_halo)

    for s in range(8):
        put_near(s, 0, npos, tiles)
    mine = tiles[SELF]
    post[...] = jnp.transpose(jnp.concatenate([mine] * (LANES // TILE), axis=0))
    for q, (x, y, z) in enumerate(CELLS):
        high, low = halves(feats[SELF, x, y, z])
        put_forward(high, low, fown, q * SLOTS, LANES)
        put_backward(high, low, bown, q * SLOTS, LANES)
    for copy in held[3:]:
        copy.wait()

    def own_pairs(s, b):
        near_pairs(s, 0, npos, post, geo, rad, opair[b], 0, LANES)

    def own_moments(s, b):
        mom[b][...] = dot(opair[b][...], fown[...])
        for m in range(9):
            summed[m, own_rows(s), :] = weighted(mom[b], radial, m)

    over_cells(0, 8, own_pairs, own_moments)
    pl.when(early)(send_halo)

    def ghost_pairs(s, b):
        for chunk in range(1, CHUNKS):
            at = (chunk - 1) * LANES
            near_pairs(s, chunk, npos, post, geo, rad, pair[b], at, GHOST + at)

    def ghost_moments(s, b):
        mom[b][...] = dot(pair[b][...], fcat[s])
        for m in range(9):
            summed[m, own_rows(s), :] = summed[m, own_rows(s), :] + weighted(mom[b], radial, m)

    def ghost_gradients(s, b):
        gradient_pairs(s, summed, radial, gpair[b])
        dpair[b][...] = dot(gpair[b][...], bcat[s], 1)

    def ghost_forces(s, b):
        pull = None
        for chunk in range(1, CHUNKS):
            at = (chunk - 1) * LANES
            more = chunk_forces(s, chunk, dpair[b], at, GHOST + at, geo, rad, ngrad)
            pull = more if pull is None else [p + q for p, q in zip(pull, more)]
        for a in range(3):
            center[a, own_rows(s), :] = pull[a]

    returns = {
        domain: pltpu.make_async_remote_copy(
            grads.at[domain], landed.at[26 - domain], back_sends.at[domain],
            back_recvs.at[26 - domain], device_id=neighbour(domain), device_id_type=MESH,
        )
        for domain in range(27)
        if domain != SELF
    }
    for half in (1, 0):
        coming = [
            pieces for domain, pieces in halo.items() if (side(domain) == 1) == (half == 0)
        ]
        for positions, _ in coming:
            positions.wait_recv()
        for s in range(4 * half, 4 * half + 4):
            for chunk in range(1, CHUNKS):
                put_near(s, chunk, npos, tiles)
        if half == 1:
            over_cells(4, 4, ghost_pairs)
        for _, features in coming:
            features.wait_recv()
        for s in range(4 * half, 4 * half + 4):
            filled = {(c, p): (domain, q) for c, p, domain, q in TABLES[s]}
            for chunk in range(1, CHUNKS):
                for place in range(8):
                    at = (chunk - 1) * LANES + place * SLOTS
                    if (chunk, place) in filled:
                        domain, q = filled[(chunk, place)]
                        high, low = halves(feats[(domain,) + CELLS[q]])
                    else:
                        high = low = jnp.zeros((SLOTS, LANES), BF16)
                    put_forward(high, low, fcat.at[s], at, GHOST)
                    put_backward(high, low, bcat.at[s], at, GHOST)
        if half == 1:
            over_cells(4, 4, ghost_moments)
        else:
            over_cells(0, 4, ghost_pairs, ghost_moments)
        mix_half(half, slot, counts, mix, readout, summed, layers)
        over_cells(4 * half, 4, ghost_gradients, ghost_forces)
        for s in range(4 * half, 4 * half + 4):
            for chunk in range(1, CHUNKS):
                scatter(s, chunk, ngrad, grads)
        for domain, copy in returns.items():
            if (side(domain) == 1) == (half == 1):
                copy.start()

    def own_gradients(s, b):
        gradient_pairs(s, summed, radial, gpair[b])
        odpair[b][...] = dot(gpair[b][...], bown[...], 1)

    def own_forces(s, b):
        pull = chunk_forces(s, 0, odpair[b], 0, LANES, geo, rad, ngrad)
        for a in range(3):
            center[a, own_rows(s), :] = center[a, own_rows(s), :] + pull[a]

    over_cells(0, 8, own_gradients, own_forces)
    for s in range(8):
        scatter(s, 0, ngrad, grads)
    total = grads[SELF]
    pulls = [jnp.sum(jnp.transpose(center[a]), axis=0, keepdims=True) for a in range(3)]
    total = total - jnp.concatenate(pulls + [jnp.zeros((TILE - 3, LANES), F32)], axis=0)

    layer = jnp.sum(jnp.transpose(layers[...]), axis=0, keepdims=True)
    lane16 = lax.broadcasted_iota(jnp.int32, (1, SLOTS), 1)
    for q, (x, y, z) in enumerate(CELLS):
        kind = species[x, y, z : z + 1, :]
        value = layer[:, q * SLOTS : (q + 1) * SLOTS]
        for k in range(table.shape[0]):
            value = value + jnp.where(kind == k, table[k], 0.0)
        occupied = lane16 < counts[x, y : y + 1, z : z + 1]
        energy_ref[x, y, z : z + 1, :] = jnp.where(occupied, value, 0.0)

    for domain, copy in returns.items():
        copy.wait_recv()
        total = total + landed[26 - domain]
    total = -total
    for q, (x, y, z) in enumerate(CELLS):
        force_ref[x, y, :, z, :] = total[0:3, q * SLOTS : (q + 1) * SLOTS]
    for domain, pieces in halo.items():
        for copy in pieces + (returns[domain],):
            copy.wait_send()


VMEM = pl.BlockSpec(memory_space=pltpu.VMEM)
HBM = pl.BlockSpec(memory_space=pltpu.HBM)


def per_device(positions, features, species, counts, species_energy, radial_weight, mix_weight, readout):
    energies, forces = pl.pallas_call(
        whole_kernel,
        out_shape=(
            jax.ShapeDtypeStruct((2, 2, 2, SLOTS), F32),
            jax.ShapeDtypeStruct((2, 2, 3, 2, SLOTS), F32),
        ),
        in_specs=[HBM] * 8,
        out_specs=(VMEM, VMEM),
        scratch_shapes=[
            pltpu.VMEM((2, 2, 3, 2, SLOTS), F32),
            pltpu.VMEM((2, 2, 2, SLOTS, LANES), F32),
            pltpu.VMEM((2, 2, 2, SLOTS), jnp.int32),
            pltpu.VMEM((2, 2, 2), jnp.int32),
            pltpu.SMEM(species_energy.shape, F32),
            pltpu.VMEM((3, BASIS, LANES), F32),
            pltpu.VMEM((3, LANES, LANES), F32),
            pltpu.VMEM((4, LANES), F32),
            pltpu.SemaphoreType.DMA((8,)),
            pltpu.VMEM((27, TILE, LANES), F32),
            pltpu.VMEM((27, 2, 2, 2, SLOTS, LANES), F32),
            pltpu.SemaphoreType.DMA((2, 27)),
            pltpu.SemaphoreType.DMA((2, 27)),
            pltpu.VMEM((27, TILE, LANES), F32),
            pltpu.SemaphoreType.DMA((27,)),
            pltpu.SemaphoreType.DMA((27,)),
            pltpu.VMEM((8, TILE, NEAR), F32),
            pltpu.VMEM((LANES, LANES), F32),
            pltpu.VMEM((2 * LANES, 256), BF16),
            pltpu.VMEM((8, 2 * GHOST, 256), BF16),
            pltpu.VMEM((2 * LANES, 256), BF16),
            pltpu.VMEM((8, 2 * GHOST, 256), BF16),
            pltpu.VMEM((9, LANES, LANES), F32),
            pltpu.VMEM((LANES, LANES), F32),
            pltpu.VMEM((8, 2 * BASIS, SLOTS, NEAR), F32),
            pltpu.VMEM((8, 4, SLOTS, NEAR), F32),
            pltpu.VMEM((8, TILE, NEAR), F32),
            pltpu.VMEM((3, LANES, LANES), F32),
            pltpu.VMEM((27, TILE, LANES), F32),
            *[pltpu.VMEM((ROWS, 2 * LANES), BF16)] * STEP,
            *[pltpu.VMEM((ROWS, 2 * GHOST), BF16)] * STEP,
            *[pltpu.VMEM((ROWS, 256), F32)] * STEP,
            *[pltpu.VMEM((ROWS, 256), BF16)] * STEP,
            *[pltpu.VMEM((ROWS, 2 * LANES), F32)] * STEP,
            *[pltpu.VMEM((ROWS, 2 * GHOST), F32)] * STEP,
        ],
        compiler_params=pltpu.CompilerParams(
            collective_id=0, has_side_effects=True, vmem_limit_bytes=60 * 2**20
        ),
    )(
        jnp.swapaxes(positions, 2, 3), features, species, counts, species_energy,
        jnp.swapaxes(radial_weight, 0, 1), mix_weight, readout,
    )
    return energies, jnp.swapaxes(forces, 2, 3)


def solution(mesh):
    grid = P("gx", "gy", "gz")
    return jax.shard_map(
        per_device,
        mesh=mesh,
        in_specs=(grid, grid, grid, grid, P(), P(), P(), P()),
        out_specs=(grid, grid),
        check_vma=False,
    )
```

```python
import math

import jax
import jax.numpy as jnp
import numpy as np
from jax import lax
from jax.experimental import pallas as pl
from jax.experimental.pallas import tpu as pltpu
from jax.sharding import PartitionSpec as P

CUTOFF = 5.0
CELL_SIDE = 5.0
SOFTENING = 0.5
BASIS = 8
SLOTS = 16
LANES = 128
CHUNKS = 4
NEAR = CHUNKS * LANES
GHOST = NEAR - LANES
STEP = 4
TILE = 4
ROWS = BASIS * 9 * SLOTS
DEGREE_OF = (0, 1, 1, 1, 2, 2, 2, 2, 2)
SELF = 13
MESH = pl.DeviceIdType.MESH
AXES = ("gx", "gy", "gz")
R3, R5, R15 = math.sqrt(3.0), math.sqrt(5.0), math.sqrt(15.0)
F32, BF16 = jnp.float32, jnp.bfloat16

OFFSETS = [(a, b, c) for a in (-1, 0, 1) for b in (-1, 0, 1) for c in (-1, 0, 1)]
CELLS = [(x, y, z) for x in (0, 1) for y in (0, 1) for z in (0, 1)]


def near_table(cell):
    sign = [1 if c == 1 else -1 for c in cell]
    rim = [0 if s == 1 else 1 for s in sign]
    taken = {(0, q) for q in range(8)}
    table = [(0, q, SELF, q) for q in range(8)]
    late = []
    for size in (1, 2, 3):
        for subset in range(1, 8):
            dims = [d for d in range(3) if subset >> d & 1]
            if len(dims) != size:
                continue
            off = [sign[d] if d in dims else 0 for d in range(3)]
            domain = OFFSETS.index(tuple(off))
            for q, coords in enumerate(CELLS):
                if any(coords[d] != rim[d] for d in dims):
                    continue
                for chunk in range(1, CHUNKS):
                    if (chunk, q) not in taken:
                        taken.add((chunk, q))
                        table.append((chunk, q, domain, q))
                        break
                else:
                    late.append((domain, q))
    for domain, q in late:
        chunk, place = min(
            (c, p) for c in range(1, CHUNKS) for p in range(8) if (c, p) not in taken
        )
        taken.add((chunk, place))
        table.append((chunk, place, domain, q))
    return table


TABLES = [near_table(cell) for cell in CELLS]


def grouped(table, chunk):
    groups = {}
    for c, place, domain, q in table:
        if c == chunk:
            groups.setdefault((domain, (place - q) % 8), []).append(place)
    return sorted(groups.items())


def places_mask(places):
    lane = lax.broadcasted_iota(jnp.int32, (TILE, LANES), 1)
    mask = None
    for place in places:
        one = (lane >= place * SLOTS) & (lane < (place + 1) * SLOTS)
        mask = one if mask is None else mask | one
    return mask


def neighbour(domain):
    place = []
    for axis, step in zip(AXES, OFFSETS[domain]):
        count = lax.axis_size(axis)
        place.append(lax.rem(lax.axis_index(axis) + step + count, count))
    return tuple(place)


def side(domain):
    return OFFSETS[domain][0]


def rim_of(domain):
    return tuple(
        pl.ds(0, 2) if step == 0 else pl.ds(1 if step == 1 else 0, 1) for step in OFFSETS[domain]
    )


def greet():
    barrier = pltpu.get_barrier_semaphore()
    for domain in range(27):
        if domain != SELF:
            pl.semaphore_signal(
                barrier, inc=1, device_id=neighbour(domain), device_id_type=MESH
            )
    return barrier


def halves(value):
    high = value.astype(BF16)
    return high, (value - high.astype(F32)).astype(BF16)


def dot(a, b, rhs_dim=0):
    return lax.dot_general(
        a, b, (((1,), (rhs_dim,)), ((), ())), preferred_element_type=F32
    )


def dot_split(a, b, rhs_dim=0):
    a_high, a_low = halves(a)
    b_high, b_low = halves(b)
    return (
        dot(a_low, b_high, rhs_dim) + dot(a_high, b_low, rhs_dim) + dot(a_high, b_high, rhs_dim)
    )


def harmonics(ux, uy, uz):
    square = ux * ux + uy * uy + uz * uz
    return [
        None,
        R3 * ux,
        R3 * uy,
        R3 * uz,
        R15 * ux * uy,
        R15 * uy * uz,
        0.5 * R5 * (3.0 * uz * uz - square),
        R15 * ux * uz,
        0.5 * R15 * (ux * ux - uy * uy),
    ]


def radial_parts(distance, inverse, keep):
    t = jnp.minimum(distance * (1.0 / CUTOFF), 1.0)
    phi = math.pi * (t - 0.5)
    sq = phi * phi
    sine, cosine = 0.0, 0.0
    for k in range(6, -1, -1):
        if k < 6:
            sine = sine * sq + (-1) ** k / math.factorial(2 * k + 1)
        cosine = cosine * sq + (-1) ** k / math.factorial(2 * k)
    s1, c1 = cosine, -(sine * phi)
    t2 = t * t
    t4 = t2 * t2
    env = jnp.where(keep, 1.0 + t4 * t * (-21.0 + t * (35.0 - 15.0 * t)), 0.0)
    gap = 1.0 - t
    env_d = jnp.where(keep, (-105.0 / CUTOFF) * t4 * gap * gap, 0.0)
    scale = math.sqrt(2.0 / CUTOFF)
    w = scale * env * inverse
    w_d = inverse * (scale * env_d - w)
    twice = 2.0 * c1
    sines, cosines = [s1], [c1]
    for n in range(1, BASIS):
        sines.append(twice * sines[-1] - (sines[-2] if n > 1 else 0.0))
        cosines.append(twice * cosines[-1] - (cosines[-2] if n > 1 else 1.0))
    values = [s * w for s in sines]
    slopes = [
        ((n + 1) * math.pi / CUTOFF) * (c * w) + s * w_d
        for n, (s, c) in enumerate(zip(sines, cosines))
    ]
    return values, slopes


def near_pairs(s, chunk, npos, post, geo, rad, pair, high_at, low_at):
    own = pl.ds(pl.multiple_of(s * SLOTS, SLOTS), SLOTS)
    at = slice(chunk * LANES, (chunk + 1) * LANES)
    rx, ry, rz = (npos[s, a : a + 1, at] - post[own, a : a + 1] for a in range(3))
    squared = rx * rx + ry * ry + rz * rz + SOFTENING * SOFTENING
    inverse = lax.rsqrt(squared)
    distance = squared * inverse
    keep = distance < CUTOFF
    if chunk == 0:
        lane = lax.broadcasted_iota(jnp.int32, (SLOTS, LANES), 1)
        slot = lax.broadcasted_iota(jnp.int32, (SLOTS, LANES), 0)
        keep = keep & (lane != slot + s * SLOTS)
    values, slopes = radial_parts(distance, inverse, keep)
    ux, uy, uz = rx * inverse, ry * inverse, rz * inverse
    for a, part in enumerate((ux, uy, uz, inverse)):
        geo[s, a, :, at] = part
    harmonic = harmonics(ux, uy, uz)
    for n in range(BASIS):
        rad[s, n, :, at] = values[n]
        rad[s, BASIS + n, :, at] = slopes[n]
        for m in range(9):
            high, low = halves(values[n] if m == 0 else values[n] * harmonic[m])
            rows = slice((n * 9 + m) * SLOTS, (n * 9 + m + 1) * SLOTS)
            pair[rows, high_at : high_at + LANES] = high
            pair[rows, low_at : low_at + LANES] = low


def weighted(mom, radial, m):
    total = None
    for n in range(BASIS):
        rows = slice((n * 9 + m) * SLOTS, (n * 9 + m + 1) * SLOTS)
        l = DEGREE_OF[m]
        term = (mom[rows, 0:128] + mom[rows, 128:256]) * radial[l, n : n + 1, :]
        total = term if total is None else total + term
    return total


def put_near(s, chunk, npos, tiles):
    row = lax.broadcasted_iota(jnp.int32, (TILE, LANES), 0)
    value = jnp.full((TILE, LANES), 100.0, F32)
    for (domain, turn), places in grouped(TABLES[s], chunk):
        ox, oy, oz = (2.0 * CELL_SIDE * o for o in OFFSETS[domain])
        piece = tiles[domain]
        if domain != SELF:
            piece = piece + jnp.where(row == 0, ox, jnp.where(row == 1, oy, oz))
        if turn:
            piece = pltpu.roll(piece, turn * SLOTS, 1)
        value = piece if len(places) == 8 else jnp.where(places_mask(places), piece, value)
    npos[s, :, chunk * LANES : (chunk + 1) * LANES] = value


def put_forward(high, low, fcat, at, low_by):
    rows, low_rows = slice(at, at + SLOTS), slice(at + low_by, at + low_by + SLOTS)
    fcat[rows, 0:128] = high
    fcat[rows, 128:256] = low
    fcat[low_rows, 0:128] = high
    fcat[low_rows, 128:256] = jnp.zeros_like(low)


def put_backward(high, low, fback, at, low_by):
    rows, low_rows = slice(at, at + SLOTS), slice(at + low_by, at + low_by + SLOTS)
    fback[rows, 0:128] = high
    fback[rows, 128:256] = high
    fback[low_rows, 0:128] = low
    fback[low_rows, 128:256] = jnp.zeros_like(low)


def own_rows(s):
    return pl.ds(pl.multiple_of(s * SLOTS, SLOTS), SLOTS)


def over_cells(first, count, *works):
    def step(t, carry):
        s = first + STEP * t
        for work in works:
            for b in range(STEP):
                work(s + b, b)
        return carry

    lax.fori_loop(0, count // STEP, step, 0)


def gradient_pairs(s, summed, radial, gpair):
    for m in range(9):
        slope = summed[m, own_rows(s), :]
        l = DEGREE_OF[m]
        for n in range(BASIS):
            rows = slice((n * 9 + m) * SLOTS, (n * 9 + m + 1) * SLOTS)
            high, low = halves(slope * radial[l, n : n + 1, :])
            gpair[rows, 0:128] = high
            gpair[rows, 128:256] = low


def chunk_forces(s, chunk, dpair, high_at, low_at, geo, rad, ngrad):
    at = slice(chunk * LANES, (chunk + 1) * LANES)
    ux, uy, uz, inverse = (geo[s, a, :, at] for a in range(4))
    harmonic = harmonics(ux, uy, uz)
    amp = [None] * 9
    along = None
    for n in range(BASIS):
        value, slope = rad[s, n, :, at], rad[s, BASIS + n, :, at]
        inner = None
        for m in range(9):
            rows = slice((n * 9 + m) * SLOTS, (n * 9 + m + 1) * SLOTS)
            part = dpair[rows, high_at : high_at + LANES] + dpair[rows, low_at : low_at + LANES]
            if m > 0:
                amp[m] = part * value if n == 0 else amp[m] + part * value
            inner = part if m == 0 else inner + part * harmonic[m]
        along = inner * slope if n == 0 else along + inner * slope
    vx = R3 * amp[1] + R15 * (uy * amp[4] + uz * amp[7] + ux * amp[8]) - R5 * (ux * amp[6])
    vy = R3 * amp[2] + R15 * (ux * amp[4] + uz * amp[5] - uy * amp[8]) - R5 * (uy * amp[6])
    vz = R3 * amp[3] + R15 * (uy * amp[5] + ux * amp[7]) + (2.0 * R5) * (uz * amp[6])
    central = along - inverse * (ux * vx + uy * vy + uz * vz)
    slopes = [u * central + inverse * v for u, v in ((ux, vx), (uy, vy), (uz, vz))]
    for a in range(3):
        ngrad[s, a : a + 1, at] = jnp.sum(slopes[a], axis=0, keepdims=True)
    return slopes


def scatter(s, chunk, ngrad, grads):
    whole = ngrad[s, :, chunk * LANES : (chunk + 1) * LANES]
    for (domain, turn), places in grouped(TABLES[s], chunk):
        piece = whole if len(places) == 8 else jnp.where(places_mask(places), whole, 0.0)
        if turn:
            piece = pltpu.roll(piece, (8 - turn) * SLOTS, 1)
        grads[domain] = grads[domain] + piece


SPANS = (slice(0, 1), slice(1, 4), slice(4, 9))


def mix_half(half, slot, counts, mix, readout, summed, layers):
    rows = slice(half * 64, (half + 1) * 64)
    occupied = jnp.concatenate(
        [
            jnp.where(slot < counts[half, y : y + 1, z : z + 1], 1.0, 0.0)
            for y in (0, 1)
            for z in (0, 1)
        ],
        axis=0,
    )
    mixed = []
    for l, span in enumerate(SPANS):
        size = span.stop - span.start
        part = dot_split(summed[span, rows].reshape(size * 64, LANES), mix[l])
        mixed += [part[i * 64 : (i + 1) * 64] for i in range(size)]
    q0 = mixed[0]
    q1 = sum(v * v for v in mixed[1:4])
    q2 = sum(v * v for v in mixed[4:9])
    r0, r1, r2, r3 = (readout[i : i + 1, :] for i in range(4))
    layers[rows] = q0 * r0 + q1 * r1 + q2 * r2 + (q0 * q1) * r3
    slope1 = 2.0 * occupied * (r1 + q0 * r3)
    slope2 = 2.0 * occupied * r2
    back = [occupied * (r0 + q1 * r3)]
    back += [v * slope1 for v in mixed[1:4]]
    back += [v * slope2 for v in mixed[4:9]]
    for l, span in enumerate(SPANS):
        part = dot_split(jnp.concatenate(back[span], axis=0), mix[l], 1)
        summed[span, rows] = part.reshape(span.stop - span.start, 64, LANES)


def whole_kernel(
    pos_hbm, feat_hbm, species_hbm, counts_hbm, table_hbm, radial_hbm, mix_hbm, readout_hbm,
    energy_ref, force_ref,
    pos, feat, species, counts, table, radial, mix, readout, loads,
    tiles, feats, sends, recvs, landed, back_sends, back_recvs,
    npos, post, fown, fcat, bown, bcat, summed, layers, rad, geo, ngrad, center, grads,
    *buffers,
):
    opair, pair, mom, gpair, odpair, dpair = (
        buffers[i * STEP : (i + 1) * STEP] for i in range(6)
    )
    held = [
        pltpu.make_async_copy(source, target, loads.at[i])
        for i, (source, target) in enumerate(
            (
                (pos_hbm, pos), (counts_hbm, counts), (feat_hbm, feat), (radial_hbm, radial),
                (mix_hbm, mix), (readout_hbm, readout), (species_hbm, species), (table_hbm, table),
            )
        )
    ]
    for copy in held[:3]:
        copy.start()
    barrier = greet()
    for copy in held[3:]:
        copy.start()
    slot = lax.broadcasted_iota(jnp.int32, (SLOTS, LANES), 0)
    tiles[SELF] = jnp.zeros((TILE, LANES), F32)
    ngrad[...] = jnp.zeros_like(ngrad)
    grads[...] = jnp.zeros_like(grads)
    for copy in held[:3]:
        copy.wait()
    for q, (x, y, z) in enumerate(CELLS):
        tiles[SELF, 0:3, q * SLOTS : (q + 1) * SLOTS] = pos[x, y, :, z, :]
        occupied = slot < counts[x, y : y + 1, z : z + 1]
        feats[SELF, x, y, z] = jnp.where(occupied, feat[x, y, z], 0.0)
    lane = lax.broadcasted_iota(jnp.int32, (TILE, LANES), 1)
    row = lax.broadcasted_iota(jnp.int32, (TILE, LANES), 0)
    shift = jnp.where(row == 0, lane // 64, jnp.where(row == 1, lane // 32 % 2, lane // 16 % 2))
    tiles[SELF] = tiles[SELF] + CELL_SIDE * shift.astype(F32)

    halo = {}
    for domain in range(27):
        if domain == SELF:
            continue
        there, rim, back = neighbour(domain), rim_of(domain), 26 - domain
        halo[domain] = (
            pltpu.make_async_remote_copy(
                tiles.at[SELF], tiles.at[back], sends.at[0, domain], recvs.at[0, back],
                device_id=there, device_id_type=MESH,
            ),
            pltpu.make_async_remote_copy(
                feats.at[(SELF,) + rim], feats.at[(back,) + rim], sends.at[1, domain],
                recvs.at[1, back], device_id=there, device_id_type=MESH,
            ),
        )

    def send_halo():
        pl.semaphore_wait(barrier, 26)
        for piece in (0, 1):
            for step in (-1, 0, 1):
                for domain, pieces in halo.items():
                    if side(domain) == step:
                        pieces[piece].start()

    planes = max(lax.axis_size("gx") // 2, 1)
    early = lax.rem(lax.axis_index("gx"), planes) == 0
    pl.when(jnp.logical_not(early))(send_halo)

    for s in range(8):
        put_near(s, 0, npos, tiles)
    mine = tiles[SELF]
    post[...] = jnp.transpose(jnp.concatenate([mine] * (LANES // TILE), axis=0))
    for q, (x, y, z) in enumerate(CELLS):
        high, low = halves(feats[SELF, x, y, z])
        put_forward(high, low, fown, q * SLOTS, LANES)
        put_backward(high, low, bown, q * SLOTS, LANES)
    for copy in held[3:]:
        copy.wait()

    def own_pairs(s, b):
        near_pairs(s, 0, npos, post, geo, rad, opair[b], 0, LANES)

    def own_moments(s, b):
        mom[b][...] = dot(opair[b][...], fown[...])
        for m in range(9):
            summed[m, own_rows(s), :] = weighted(mom[b], radial, m)

    over_cells(0, 8, own_pairs, own_moments)
    pl.when(early)(send_halo)

    def ghost_pairs(s, b):
        for chunk in range(1, CHUNKS):
            at = (chunk - 1) * LANES
            near_pairs(s, chunk, npos, post, geo, rad, pair[b], at, GHOST + at)

    def ghost_moments(s, b):
        mom[b][...] = dot(pair[b][...], fcat[s])
        for m in range(9):
            summed[m, own_rows(s), :] = summed[m, own_rows(s), :] + weighted(mom[b], radial, m)

    def ghost_gradients(s, b):
        gradient_pairs(s, summed, radial, gpair[b])
        dpair[b][...] = dot(gpair[b][...], bcat[s], 1)

    def ghost_forces(s, b):
        pull = None
        for chunk in range(1, CHUNKS):
            at = (chunk - 1) * LANES
            more = chunk_forces(s, chunk, dpair[b], at, GHOST + at, geo, rad, ngrad)
            pull = more if pull is None else [p + q for p, q in zip(pull, more)]
        for a in range(3):
            center[a, own_rows(s), :] = pull[a]

    returns = {
        domain: pltpu.make_async_remote_copy(
            grads.at[domain], landed.at[26 - domain], back_sends.at[domain],
            back_recvs.at[26 - domain], device_id=neighbour(domain), device_id_type=MESH,
        )
        for domain in range(27)
        if domain != SELF
    }
    for half in (1, 0):
        coming = [
            pieces for domain, pieces in halo.items() if (side(domain) == 1) == (half == 0)
        ]
        for positions, _ in coming:
            positions.wait_recv()
        for s in range(4 * half, 4 * half + 4):
            for chunk in range(1, CHUNKS):
                put_near(s, chunk, npos, tiles)
        if half == 1:
            over_cells(4, 4, ghost_pairs)
        for _, features in coming:
            features.wait_recv()
        for s in range(4 * half, 4 * half + 4):
            filled = {(c, p): (domain, q) for c, p, domain, q in TABLES[s]}
            for chunk in range(1, CHUNKS):
                for place in range(8):
                    at = (chunk - 1) * LANES + place * SLOTS
                    if (chunk, place) in filled:
                        domain, q = filled[(chunk, place)]
                        high, low = halves(feats[(domain,) + CELLS[q]])
                    else:
                        high = low = jnp.zeros((SLOTS, LANES), BF16)
                    put_forward(high, low, fcat.at[s], at, GHOST)
                    put_backward(high, low, bcat.at[s], at, GHOST)
        if half == 1:
            over_cells(4, 4, ghost_moments)
        else:
            over_cells(0, 4, ghost_pairs, ghost_moments)
        mix_half(half, slot, counts, mix, readout, summed, layers)
        over_cells(4 * half, 4, ghost_gradients, ghost_forces)
        for s in range(4 * half, 4 * half + 4):
            for chunk in range(1, CHUNKS):
                scatter(s, chunk, ngrad, grads)
        for domain, copy in returns.items():
            if (side(domain) == 1) == (half == 1):
                copy.start()

    def own_gradients(s, b):
        gradient_pairs(s, summed, radial, gpair[b])
        odpair[b][...] = dot(gpair[b][...], bown[...], 1)

    def own_forces(s, b):
        pull = chunk_forces(s, 0, odpair[b], 0, LANES, geo, rad, ngrad)
        for a in range(3):
            center[a, own_rows(s), :] = center[a, own_rows(s), :] + pull[a]

    over_cells(0, 8, own_gradients, own_forces)
    for s in range(8):
        scatter(s, 0, ngrad, grads)
    total = grads[SELF]
    pulls = [jnp.sum(jnp.transpose(center[a]), axis=0, keepdims=True) for a in range(3)]
    total = total - jnp.concatenate(pulls + [jnp.zeros((TILE - 3, LANES), F32)], axis=0)

    layer = jnp.sum(jnp.transpose(layers[...]), axis=0, keepdims=True)
    lane16 = lax.broadcasted_iota(jnp.int32, (1, SLOTS), 1)
    for q, (x, y, z) in enumerate(CELLS):
        kind = species[x, y, z : z + 1, :]
        value = layer[:, q * SLOTS : (q + 1) * SLOTS]
        for k in range(table.shape[0]):
            value = value + jnp.where(kind == k, table[k], 0.0)
        occupied = lane16 < counts[x, y : y + 1, z : z + 1]
        energy_ref[x, y, z : z + 1, :] = jnp.where(occupied, value, 0.0)

    for domain, copy in returns.items():
        copy.wait_recv()
        total = total + landed[26 - domain]
    total = -total
    for q, (x, y, z) in enumerate(CELLS):
        force_ref[x, y, :, z, :] = total[0:3, q * SLOTS : (q + 1) * SLOTS]
    for domain, pieces in halo.items():
        for copy in pieces + (returns[domain],):
            copy.wait_send()


VMEM = pl.BlockSpec(memory_space=pltpu.VMEM)
HBM = pl.BlockSpec(memory_space=pltpu.HBM)


def per_device(positions, features, species, counts, species_energy, radial_weight, mix_weight, readout):
    energies, forces = pl.pallas_call(
        whole_kernel,
        out_shape=(
            jax.ShapeDtypeStruct((2, 2, 2, SLOTS), F32),
            jax.ShapeDtypeStruct((2, 2, 3, 2, SLOTS), F32),
        ),
        in_specs=[HBM] * 8,
        out_specs=(VMEM, VMEM),
        scratch_shapes=[
            pltpu.VMEM((2, 2, 3, 2, SLOTS), F32),
            pltpu.VMEM((2, 2, 2, SLOTS, LANES), F32),
            pltpu.VMEM((2, 2, 2, SLOTS), jnp.int32),
            pltpu.VMEM((2, 2, 2), jnp.int32),
            pltpu.SMEM(species_energy.shape, F32),
            pltpu.VMEM((3, BASIS, LANES), F32),
            pltpu.VMEM((3, LANES, LANES), F32),
            pltpu.VMEM((4, LANES), F32),
            pltpu.SemaphoreType.DMA((8,)),
            pltpu.VMEM((27, TILE, LANES), F32),
            pltpu.VMEM((27, 2, 2, 2, SLOTS, LANES), F32),
            pltpu.SemaphoreType.DMA((2, 27)),
            pltpu.SemaphoreType.DMA((2, 27)),
            pltpu.VMEM((27, TILE, LANES), F32),
            pltpu.SemaphoreType.DMA((27,)),
            pltpu.SemaphoreType.DMA((27,)),
            pltpu.VMEM((8, TILE, NEAR), F32),
            pltpu.VMEM((LANES, LANES), F32),
            pltpu.VMEM((2 * LANES, 256), BF16),
            pltpu.VMEM((8, 2 * GHOST, 256), BF16),
            pltpu.VMEM((2 * LANES, 256), BF16),
            pltpu.VMEM((8, 2 * GHOST, 256), BF16),
            pltpu.VMEM((9, LANES, LANES), F32),
            pltpu.VMEM((LANES, LANES), F32),
            pltpu.VMEM((8, 2 * BASIS, SLOTS, NEAR), F32),
            pltpu.VMEM((8, 4, SLOTS, NEAR), F32),
            pltpu.VMEM((8, TILE, NEAR), F32),
            pltpu.VMEM((3, LANES, LANES), F32),
            pltpu.VMEM((27, TILE, LANES), F32),
            *[pltpu.VMEM((ROWS, 2 * LANES), BF16)] * STEP,
            *[pltpu.VMEM((ROWS, 2 * GHOST), BF16)] * STEP,
            *[pltpu.VMEM((ROWS, 256), F32)] * STEP,
            *[pltpu.VMEM((ROWS, 256), BF16)] * STEP,
            *[pltpu.VMEM((ROWS, 2 * LANES), F32)] * STEP,
            *[pltpu.VMEM((ROWS, 2 * GHOST), F32)] * STEP,
        ],
        compiler_params=pltpu.CompilerParams(
            collective_id=0, has_side_effects=True, vmem_limit_bytes=60 * 2**20
        ),
    )(
        jnp.swapaxes(positions, 2, 3), features, species, counts, species_energy,
        jnp.swapaxes(radial_weight, 0, 1), mix_weight, readout,
    )
    return energies, jnp.swapaxes(forces, 2, 3)


def solution(mesh):
    grid = P("gx", "gy", "gz")
    return jax.shard_map(
        per_device,
        mesh=mesh,
        in_specs=(grid, grid, grid, grid, P(), P(), P(), P()),
        out_specs=(grid, grid),
        check_vma=False,
    )
```
